32 devices in a mesh: groups: 2 (over y), layer: 4 (over z), token: 2 (over x), width: 2 (over core).
Axes of the slice: x: 2, y: 2, z: 4, core: 2. Of those that a mesh axis runs over, the one named last changes fastest.
Arguments:
- source_acts: bfloat16 [8, 1024, 4096], P('layer', 'groups', ('token', 'width')), parts along dimension 1, may hold values from -6 to 6
- enc_weight: bfloat16 [8, 4096, 128], P('layer', ('token', 'width')), may hold values from -0.09375 to 0.09375
- enc_offset: float32 [8, 128], P('layer'), may hold values from -4 to 4
- topk_latents: int32 [8, 1024, 64], P('layer', 'groups'), parts along dimension 1, may hold values from 0 to 127, all different within a row
- pair_table: int32 [36, 2], P('layer'), may hold values from 0 to 7, as said below
- dec_weight: bfloat16 [36, 128, 4096], P('layer', None, ('token', 'width')), may hold values from -0.25 to 0.25
- target_acts: bfloat16 [8, 1024, 4096], P('layer', 'groups', ('token', 'width')), parts along dimension 1, may hold values from -6 to 6
Outputs:
- dec_gradient: bfloat16 [72, 128, 4096], P(('groups', 'layer'), None, ('token', 'width')), parts along dimension 0
- enc_gradient: float32 [16, 4096, 128], P(('groups', 'layer'), ('token', 'width')), parts along dimension 0
The draws below stay inside these ranges and needn't reach their ends.
There are 2 independent parts, one for each index of `groups`. The reference program is written for one: setup_inputs(seed, part) draws one part's arguments, and reference() takes and returns one part's arrays. A program takes and returns all parts, laid end to end along the dimension named above; an argument that names none is the same for every part. Nothing has to cross between parts.
Inputs may be any that keep to these rules, and one draw needn't show every extreme that they name: `topk_latents`: each row names 64 different latents. `pair_table`: each pair (s, m) with s <= m appears once; every group of 9 consecutive rows holds all pairs whose target is f or 7 - f, for one f below 4, in any order.
All inputs are finite; a program needn't handle non-finite values.
Results may differ from the reference program's by a relative error of at most 0.0049.
Values may be sent and summed in bfloat16 or wider, within the bound.
A program may use at most 128 MiB of HBM per device.

```python
import jax
import jax.numpy as jnp
from jax import lax

D = 4096
LATENTS = 128
TOPK = 64
TOKENS = 512
LAYERS = 8
PAIR_DEV = 9
PAIRS = 36
N_LAYER = 4


def draw_pair_table(key, part):
    key = jax.random.fold_in(key, 11)
    owners = LAYERS // 2
    folds = jax.random.permutation(jax.random.fold_in(key, 1), owners)
    slots = jnp.arange(PAIR_DEV, dtype=jnp.int32)

    def one_owner(device):
        fold_low = folds[device]
        first_part = slots <= fold_low
        source_ids = jnp.where(first_part, slots, slots - fold_low - 1)
        target_ids = jnp.where(first_part, fold_low, LAYERS - 1 - fold_low)
        order = jax.random.permutation(jax.random.fold_in(key, 100 + device), PAIR_DEV)
        return jnp.stack([source_ids[order], target_ids[order]], axis=1)
    return jax.vmap(one_owner)(jnp.arange(owners, dtype=jnp.int32)).reshape(PAIRS, 2).astype(jnp.int32)


def levels(stream_key, extent, cuts, least, high):
    def one(axis_at, shards_of):
        draws = jax.random.uniform(jax.random.fold_in(jax.random.fold_in(stream_key, 6), axis_at), (shards_of,), jnp.float32, least / len(cuts), high / len(cuts))
        return jnp.repeat(jnp.exp(draws), extent[axis_at] // shards_of).reshape((-1,) + (1,) * (len(extent) - axis_at - 1))

    loudness = one(*cuts[0])
    for cut in cuts[1:]:
        loudness = loudness * one(*cut)
    return loudness


def different_ones(stream_key, rows, count, top, lift):
    order = jax.random.permutation(jax.random.fold_in(stream_key, 1), count)
    favour = order
    for power in range(3):
        favour = favour * favour // count
    favour = favour * lift // count
    lots = jax.random.randint(jax.random.fold_in(stream_key, 2), (rows, count), 0, 4096) + favour
    holders = jax.random.permutation(jax.random.fold_in(stream_key, 3), rows)[jnp.arange(count) % rows]
    lots = jnp.where(jnp.arange(rows)[:, None] == holders[None, :], 1 << 14, lots)
    score = lots * count + jnp.arange(count)
    return lax.top_k(score.astype(jnp.int32), top)[1].astype(jnp.int32)


def noise(stream_key, shape, spread, limit, pieces=(), kind=jnp.bfloat16):
    level = levels(stream_key, shape, pieces, -0.22, 0.18) if pieces else 1.0
    drawn = jax.random.normal(stream_key, shape, jnp.float32) * spread * level
    return jnp.minimum(jnp.maximum(drawn, -limit), limit).astype(kind)


def setup_inputs(seed: int = 0, part: int = 0) -> dict:
    key_list = jax.random.split(jax.random.key(seed), 8)
    part_keys = jax.random.split(jax.random.fold_in(key_list[7], part), 8)
    return {
        "source_acts": noise(part_keys[0], (LAYERS, TOKENS, D), 1.0, 6.0, ((0, 4), (2, 4))),
        "enc_weight": noise(key_list[1], (LAYERS, D, LATENTS), D ** -0.5, 0.09375, ((0, 4), (1, 4))),
        "enc_offset": noise(key_list[2], (LAYERS, LATENTS), 1.0, 4.0, ((0, 4),), jnp.float32),
        "topk_latents": different_ones(part_keys[3], LAYERS * TOKENS, LATENTS, TOPK, 0).reshape((LAYERS, TOKENS, TOPK)),
        "pair_table": draw_pair_table(jax.random.fold_in(key_list[7], 71), part),
        "dec_weight": noise(key_list[5], (PAIRS, LATENTS, D), (4 * LATENTS) ** -0.5, 0.25, ((0, 4), (2, 4))),
        "target_acts": noise(part_keys[6], (LAYERS, TOKENS, D), 1.0, 6.0, ((0, 4), (2, 4))),
    }


grad_scale = 1.0 / 32.0


def active_mask(chosen, latent_total):
    columns = lax.broadcasted_iota(jnp.int32, (1, 1, 1, latent_total), 3)
    return jnp.sum((chosen[..., None] == columns).astype(jnp.float32), axis=2)


def reference(source_acts, enc_weight, enc_offset, topk_latents, pair_table, dec_weight, target_acts):
    preact = jnp.einsum("ltd,ldk->ltk", source_acts.astype(jnp.float32), enc_weight.astype(jnp.float32)) + enc_offset[:, None, :]
    picked = active_mask(topk_latents, LATENTS)
    latents = (picked * jax.nn.softplus(preact)).astype(jnp.bfloat16)
    tables = pair_table.reshape(N_LAYER, PAIR_DEV, 2)
    weights = dec_weight.reshape(N_LAYER, PAIR_DEV, LATENTS, D)
    goal_rows = target_acts.reshape(N_LAYER, 2, TOKENS, D)
    layer_ids = jnp.arange(LAYERS, dtype=jnp.int32)

    def owner_step(latent_grad, inputs):
        owner_table, weight, goal_block = inputs
        source_ids = owner_table[:, 0]
        target_ids = owner_table[:, 1]
        upper_slot = target_ids == jnp.max(target_ids)
        slot_mask = upper_slot.astype(jnp.float32)
        paired = latents[source_ids].astype(jnp.float32)
        weight_wide = weight.astype(jnp.float32)
        contrib = jnp.einsum("ptk,pkd->ptd", paired, weight_wide)
        higher = jnp.sum(contrib * slot_mask[:, None, None], axis=0)
        lower_sum = jnp.sum(contrib * (1.0 - slot_mask)[:, None, None], axis=0)
        rebuilt = jnp.stack([lower_sum, higher])
        error_grad = ((rebuilt - goal_block.astype(jnp.float32)) * grad_scale).astype(jnp.bfloat16)
        err_pair = jnp.where(upper_slot[:, None, None], error_grad[1][None], error_grad[0][None]).astype(jnp.float32)
        dec_part = jnp.einsum("ptk,ptd->pkd", paired, err_pair).astype(jnp.bfloat16)
        back_pair = jnp.einsum("ptd,pkd->ptk", err_pair, weight_wide)
        onehot = (source_ids[:, None] == layer_ids[None, :]).astype(jnp.float32)
        latent_grad = latent_grad + jnp.einsum("pl,ptk->ltk", onehot, back_pair, precision=lax.Precision.HIGHEST)
        return latent_grad, dec_part

    empty_grad = jnp.zeros((LAYERS, TOKENS, LATENTS), jnp.float32)
    latent_grad, dec_parts = lax.scan(owner_step, empty_grad, (tables, weights, goal_rows))
    pre_grad = (latent_grad * picked * jax.nn.sigmoid(preact)).astype(jnp.bfloat16)
    enc_gradient = jnp.einsum("ltd,ltk->ldk", source_acts.astype(jnp.float32), pre_grad.astype(jnp.float32))
    return dec_parts.reshape(PAIRS, LATENTS, D), enc_gradient
```

```python
import functools

import jax
import jax.numpy as jnp
from jax import lax
from jax.experimental import pallas as pl
from jax.experimental.pallas import tpu as pltpu
from jax.sharding import PartitionSpec as P

grad_scale = 1.0 / 32.0
MESH = pl.DeviceIdType.MESH
F32 = jnp.float32
BF16 = jnp.bfloat16


def kernel(
    dims,
    source_hbm, encw_hbm, offset_hbm, topk_hbm, table, decw_hbm, target_hbm,
    decgrad_hbm, encgrad_hbm,
    source, source_t, encw, offset, topk, decw, target,
    part, part_core, part_x, preact, picked, lat, err,
    back, back_core, back_xs, back_x, back_zs, back_z, pre_grad, dec_out, enc_out,
    high_pair, low_pair, slot_of,
    in_sem, out_sem,
    pc_s, pc_r, px_s, px_r, lz_s, lz_r, lx_s, lx_r, lc_s, lc_r,
    bc_s, bc_r, bx_s, bx_r, bz_s, bz_r, gx_s, gx_r, gc_s, gc_r,
):
    layers, n_z, n_t, own, tokens, width, latents, pairs = dims
    half = tokens // 2
    chunk = half // n_t
    z = lax.axis_index("layer")
    t = lax.axis_index("token")
    w = lax.axis_index("width")
    other = 1 - w

    def half_rows(core):
        return pl.ds(pl.multiple_of(core * half, half), half)

    def chunk_rows(tok, core):
        return pl.ds(pl.multiple_of(core * half + tok * chunk, chunk), chunk)

    def x_peer(d):
        return lax.rem(t + d, n_t)

    def z_peer(d):
        return lax.rem(z + d, n_z)

    def z_from(d):
        return lax.rem(z - d + n_z, n_z)

    def z_layers(zz):
        return pl.ds(zz * own, own)

    my_half = half_rows(w)
    my_rows = chunk_rows(t, w)
    sends = []

    def remote(src, dst, ssem, rsem, **where):
        copy = pltpu.make_async_remote_copy(
            src_ref=src, dst_ref=dst, send_sem=ssem, recv_sem=rsem,
            device_id=where, device_id_type=MESH,
        )
        copy.start()
        sends.append(copy)
        return copy

    loads = {}

    def load(name, src, dst, sem):
        loads[name] = pltpu.make_async_copy(src, dst, in_sem.at[sem])
        loads[name].start()

    for l in range(own):
        load(("s", l), source_hbm.at[l], source.at[l], 2 * l)
        load(("e", l), encw_hbm.at[l], encw.at[l], 2 * l + 1)
    load("topk", topk_hbm.at[:, my_rows], topk, 2 * own)
    load("offset", offset_hbm, offset, 2 * own + 1)
    load("decw", decw_hbm, decw.at[pl.ds(0, pairs)], 2 * own + 2)
    load("target", target_hbm, target, 2 * own + 3)

    barrier = pltpu.get_barrier_semaphore()
    pl.semaphore_signal(barrier, inc=1, device_id={"width": other}, device_id_type=MESH)
    for d in range(1, n_t):
        pl.semaphore_signal(barrier, inc=1, device_id={"token": x_peer(d)}, device_id_type=MESH)
    for d in range(1, n_z):
        pl.semaphore_signal(barrier, inc=1, device_id={"layer": z_peer(d)}, device_id_type=MESH)

    core_copies = []
    for l in range(own):
        loads[("s", l)].wait()
        loads[("e", l)].wait()
        part[l] = jnp.dot(source[l], encw[l], preferred_element_type=F32)
        if l == 0:
            pl.semaphore_wait(barrier, n_t + n_z - 1)
        core_copies.append(remote(
            part.at[l, half_rows(other)], part_core.at[l], pc_s.at[l], pc_r.at[l], width=other))
    x_copies = []
    for l in range(own):
        core_copies[l].wait_recv()
        part[l, my_half, :] = part[l, my_half, :] + part_core[l]
        for d in range(1, n_t):
            x_copies.append(remote(
                part.at[l, chunk_rows(x_peer(d), w)], part_x.at[l, d - 1],
                px_s.at[l, d - 1], px_r.at[l, d - 1], token=x_peer(d)))

    loads["topk"].wait()
    loads["offset"].wait()
    block = 32

    for l in range(own):
        @pl.loop(0, chunk // block)
        def _(i, l=l):
            rows = pl.ds(pl.multiple_of(i * block, block), block)
            ids = topk[l, rows, :]
            columns = lax.broadcasted_iota(jnp.int32, (block, latents), 1)
            hit = jnp.zeros((block, latents), F32)
            for k in range(topk.shape[2]):
                hit = jnp.where(ids[:, k : k + 1] == columns, 1.0, hit)
            picked[l, rows, :] = hit

    high_target = table[0, 1]
    for p in range(1, pairs):
        high_target = jnp.maximum(high_target, table[p, 1])
    for p in range(pairs):
        slot_of[p] = (table[p, 1] == high_target).astype(jnp.int32)

    @pl.loop(0, layers)
    def _(l):
        high = jnp.int32(pairs)
        low = jnp.int32(pairs)
        for p in range(pairs):
            same = table[p, 0] == l
            up = table[p, 1] == high_target
            high = jnp.where(jnp.logical_and(same, up), p, high)
            low = jnp.where(jnp.logical_and(same, jnp.logical_not(up)), p, low)
        high_pair[l] = high
        low_pair[l] = low

    for l in range(own):
        pre = part[l, my_rows, :] + offset[pl.ds(l, 1), :]
        for d in range(1, n_t):
            x_copies[l * (n_t - 1) + d - 1].wait_recv()
            pre = pre + part_x[l, d - 1]
        preact[l] = pre
        soft = jnp.maximum(pre, 0.0) + jnp.log1p(jnp.exp(-jnp.abs(pre)))
        lat[z * own + l, my_rows, :] = (picked[l] * soft).astype(BF16)

    z_copies = [None]
    for d in range(1, n_z):
        here = lat.at[z_layers(z), my_rows]
        z_copies.append(remote(here, here, lz_s.at[d - 1], lz_r.at[d - 1], layer=z_peer(d)))
    x_copies = []
    for j in range(n_z):
        if j:
            z_copies[j].wait_recv()
        for d in range(1, n_t):
            here = lat.at[z_layers(z_from(j)), my_rows]
            x_copies.append(remote(
                here, here, lx_s.at[j, d - 1], lx_r.at[j, d - 1], token=x_peer(d)))
    loads["decw"].wait()
    decw[pairs] = jnp.zeros((latents, width), BF16)
    core_copies = []
    for j in range(n_z):
        for d in range(1, n_t):
            x_copies[j * (n_t - 1) + d - 1].wait_recv()
        here = lat.at[z_layers(z_from(j)), my_half]
        core_copies.append(remote(here, here, lc_s.at[j], lc_r.at[j], width=other))
    for l in range(own):
        source_t[l] = source[l].T
    loads["target"].wait()
    for j in range(n_z):
        core_copies[j].wait_recv()

    tile = 256
    lows = layers // 2

    @pl.loop(0, width // tile)
    def _(n):
        cols = pl.ds(pl.multiple_of(n * tile, tile), tile)
        for slot, count, pair_of in ((1, layers, high_pair), (0, lows, low_pair)):
            acts = jnp.concatenate([lat[l] for l in range(count)], axis=1)
            weight = jnp.concatenate([decw[pair_of[l], :, cols] for l in range(count)], axis=0)
            rebuilt = jnp.dot(acts, weight, preferred_element_type=F32)
            goal = target[slot, :, cols].astype(F32)
            err[slot, :, cols] = ((rebuilt - goal) * grad_scale).astype(BF16)

    order = list(range(1, n_z)) + [0]
    core_copies = {}
    for j in order:
        zz = z_peer(j)
        weight = jnp.concatenate(
            [
                jnp.concatenate([decw[high_pair[zz * own + i]], decw[low_pair[zz * own + i]]], axis=1)
                for i in range(own)
            ],
            axis=0,
        )
        both = jnp.concatenate([err[1], err[0]], axis=1)
        spread = lax.dot_general(
            both, weight, (((1,), (1,)), ((), ())), preferred_element_type=F32)
        for i in range(own):
            back[j, i] = spread[:, i * latents : (i + 1) * latents]
        core_copies[j] = remote(
            back.at[j, :, half_rows(other)], back_core.at[j], bc_s.at[j], bc_r.at[j], width=other)
    x_copies = {}
    for j in order:
        core_copies[j].wait_recv()
        total = back[j, :, my_half, :] + back_core[j]
        back[j, :, my_half, :] = total
        back_xs[j] = total.astype(BF16)
        for d in range(1, n_t):
            rows = pl.ds(pl.multiple_of(x_peer(d) * chunk, chunk), chunk)
            x_copies[j, d] = remote(
                back_xs.at[j, :, rows], back_x.at[j, d - 1],
                bx_s.at[j, d - 1], bx_r.at[j, d - 1], token=x_peer(d))

    def dec_gradient(first, last):
        @pl.loop(first, last)
        def _(p):
            acts = lat[table[p, 0]].T
            grad = jnp.dot(acts, err[slot_of[p]], preferred_element_type=F32)
            dec_out[p] = grad.astype(BF16)
            pltpu.make_async_copy(dec_out.at[p], decgrad_hbm.at[p], out_sem.at[p]).start()

    middle = pairs // 2
    dec_gradient(0, middle)
    z_copies = {}
    for j in order:
        total = back[j, :, my_rows, :]
        for d in range(1, n_t):
            x_copies[j, d].wait_recv()
            total = total + back_x[j, d - 1].astype(F32)
        if j:
            back_zs[j - 1] = total.astype(BF16)
            z_copies[j] = remote(
                back_zs.at[j - 1], back_z.at[j - 1], bz_s.at[j - 1], bz_r.at[j - 1], layer=z_peer(j))
        else:
            mine = total
    dec_gradient(middle, pairs)
    for j in range(1, n_z):
        z_copies[j].wait_recv()
        mine = mine + back_z[j - 1].astype(F32)
    for l in range(own):
        pre_grad[l, my_rows, :] = (mine[l] * picked[l] * jax.nn.sigmoid(preact[l])).astype(BF16)

    here = pre_grad.at[:, my_rows]
    x_copies = [
        remote(here, here, gx_s.at[d - 1], gx_r.at[d - 1], token=x_peer(d)) for d in range(1, n_t)
    ]
    for copy in x_copies:
        copy.wait_recv()
    here = pre_grad.at[:, my_half]
    remote(here, here, gc_s.at[0], gc_r.at[0], width=other).wait_recv()
    for l in range(own):
        enc_out[l] = jnp.dot(source_t[l], pre_grad[l], preferred_element_type=F32)
        pltpu.make_async_copy(enc_out.at[l], encgrad_hbm.at[l], out_sem.at[pairs + l]).start()
    for copy in sends:
        copy.wait_send()

    @pl.loop(0, pairs)
    def _(p):
        pltpu.make_async_copy(dec_out.at[p], decgrad_hbm.at[p], out_sem.at[p]).wait()

    for l in range(own):
        pltpu.make_async_copy(enc_out.at[l], encgrad_hbm.at[l], out_sem.at[pairs + l]).wait()


def shards(n_z, n_t, source_acts, enc_weight, enc_offset, topk_latents, pair_table, dec_weight, target_acts):
    own, tokens, width = source_acts.shape
    latents = enc_weight.shape[2]
    pairs = pair_table.shape[0]
    topk = topk_latents.shape[2]
    layers = own * n_z
    half = tokens // 2
    chunk = half // n_t
    peers = max(n_t - 1, 1)
    others = max(n_z - 1, 1)
    dims = (layers, n_z, n_t, own, tokens, width, latents, pairs)
    dma = pltpu.SemaphoreType.DMA
    scratch = [
        pltpu.VMEM((own, tokens, width), BF16),
        pltpu.VMEM((own, width, tokens), BF16),
        pltpu.VMEM((own, width, latents), BF16),
        pltpu.VMEM((own, latents), F32),
        pltpu.VMEM((own, chunk, topk), jnp.int32),
        pltpu.VMEM((pairs + 1, latents, width), BF16),
        pltpu.VMEM((2, tokens, width), BF16),
        pltpu.VMEM((own, tokens, latents), F32),
        pltpu.VMEM((own, half, latents), F32),
        pltpu.VMEM((own, peers, chunk, latents), F32),
        pltpu.VMEM((own, chunk, latents), F32),
        pltpu.VMEM((own, chunk, latents), F32),
        pltpu.VMEM((layers, tokens, latents), BF16),
        pltpu.VMEM((2, tokens, width), BF16),
        pltpu.VMEM((n_z, own, tokens, latents), F32),
        pltpu.VMEM((n_z, own, half, latents), F32),
        pltpu.VMEM((n_z, own, half, latents), BF16),
        pltpu.VMEM((n_z, peers, own, chunk, latents), BF16),
        pltpu.VMEM((others, own, chunk, latents), BF16),
        pltpu.VMEM((others, own, chunk, latents), BF16),
        pltpu.VMEM((own, tokens, latents), BF16),
        pltpu.VMEM((pairs, latents, width), BF16),
        pltpu.VMEM((own, width, latents), F32),
        pltpu.SMEM((layers,), jnp.int32),
        pltpu.SMEM((layers,), jnp.int32),
        pltpu.SMEM((pairs,), jnp.int32),
        dma((2 * own + 4,)),
        dma((pairs + own,)),
    ]
    for shape in (
        (own,), (own, peers), (others,), (n_z, peers), (n_z,),
        (n_z,), (n_z, peers), (others,), (peers,), (1,),
    ):
        scratch += [dma(shape), dma(shape)]
    hbm = pl.BlockSpec(memory_space=pl.ANY)
    return pl.pallas_call(
        functools.partial(kernel, dims),
        out_shape=(
            jax.ShapeDtypeStruct((pairs, latents, width), BF16),
            jax.ShapeDtypeStruct((own, width, latents), F32),
        ),
        in_specs=[hbm, hbm, hbm, hbm, pl.BlockSpec(memory_space=pltpu.SMEM), hbm, hbm],
        out_specs=(hbm, hbm),
        scratch_shapes=scratch,
        compiler_params=pltpu.CompilerParams(
            collective_id=0, has_side_effects=True, vmem_limit_bytes=56 * 1024 * 1024
        ),
        cost_estimate=pl.CostEstimate(
            flops=2 * tokens * width * latents * (4 * pairs + 2 * own),
            bytes_accessed=2 * (2 * pairs * latents * width + 4 * tokens * width * own),
            transcendentals=0,
        ),
        name="transcoder_step",
    )(source_acts, enc_weight, enc_offset, topk_latents, pair_table, dec_weight, target_acts)


def solution(mesh):
    in_specs = (
        P("layer", "groups", ("token", "width")),
        P("layer", ("token", "width"), None),
        P("layer", None),
        P("layer", "groups", None),
        P("layer", None),
        P("layer", None, ("token", "width")),
        P("layer", "groups", ("token", "width")),
    )
    out_specs = (
        P(("groups", "layer"), None, ("token", "width")),
        P(("groups", "layer"), ("token", "width"), None),
    )
    body = functools.partial(shards, mesh.shape["layer"], mesh.shape["token"])
    return jax.shard_map(body, mesh=mesh, in_specs=in_specs, out_specs=out_specs, check_vma=False)
```

```python
import functools

import jax
import jax.numpy as jnp
from jax import lax
from jax.experimental import pallas as pl
from jax.experimental.pallas import tpu as pltpu
from jax.sharding import PartitionSpec as P

grad_scale = 1.0 / 32.0
MESH = pl.DeviceIdType.MESH
F32 = jnp.float32
BF16 = jnp.bfloat16


def kernel(
    dims,
    source_hbm, encw_hbm, offset_hbm, topk_hbm, table, decw_hbm, target_hbm,
    decgrad_hbm, encgrad_hbm,
    source, source_t, encw, offset, topk, decw, target,
    part, part_core, part_x, preact, picked, lat, err,
    back, back_core, back_xs, back_x, back_zs, back_z, pre_grad, dec_out, enc_out,
    high_pair, low_pair, slot_of,
    in_sem, out_sem,
    pc_s, pc_r, px_s, px_r, lz_s, lz_r, lx_s, lx_r, lc_s, lc_r,
    bc_s, bc_r, bx_s, bx_r, bz_s, bz_r, gx_s, gx_r, gc_s, gc_r,
):
    layers, n_z, n_t, own, tokens, width, latents, pairs = dims
    half = tokens // 2
    chunk = half // n_t
    z = lax.axis_index("layer")
    t = lax.axis_index("token")
    w = lax.axis_index("width")
    other = 1 - w

    def half_rows(core):
        return pl.ds(pl.multiple_of(core * half, half), half)

    def chunk_rows(tok, core):
        return pl.ds(pl.multiple_of(core * half + tok * chunk, chunk), chunk)

    def x_peer(d):
        return lax.rem(t + d, n_t)

    def z_peer(d):
        return lax.rem(z + d, n_z)

    def z_from(d):
        return lax.rem(z - d + n_z, n_z)

    def z_layers(zz):
        return pl.ds(zz * own, own)

    my_half = half_rows(w)
    my_rows = chunk_rows(t, w)
    sends = []

    def remote(src, dst, ssem, rsem, **where):
        copy = pltpu.make_async_remote_copy(
            src_ref=src, dst_ref=dst, send_sem=ssem, recv_sem=rsem,
            device_id=where, device_id_type=MESH,
        )
        copy.start()
        sends.append(copy)
        return copy

    loads = {}

    def load(name, src, dst, sem):
        loads[name] = pltpu.make_async_copy(src, dst, in_sem.at[sem])
        loads[name].start()

    for l in range(own):
        load(("s", l), source_hbm.at[l], source.at[l], 2 * l)
        load(("e", l), encw_hbm.at[l], encw.at[l], 2 * l + 1)
    load("topk", topk_hbm, topk, 2 * own)
    load("offset", offset_hbm, offset, 2 * own + 1)
    load("decw", decw_hbm, decw.at[pl.ds(0, pairs)], 2 * own + 2)
    load("target", target_hbm, target, 2 * own + 3)

    barrier = pltpu.get_barrier_semaphore()
    pl.semaphore_signal(barrier, inc=1, device_id={"width": other}, device_id_type=MESH)
    for d in range(1, n_t):
        pl.semaphore_signal(barrier, inc=1, device_id={"token": x_peer(d)}, device_id_type=MESH)
    for d in range(1, n_z):
        pl.semaphore_signal(barrier, inc=1, device_id={"layer": z_peer(d)}, device_id_type=MESH)

    core_copies = []
    for l in range(own):
        loads[("s", l)].wait()
        loads[("e", l)].wait()
        part[l] = jnp.dot(source[l], encw[l], preferred_element_type=F32)
    pl.semaphore_wait(barrier, n_t + n_z - 1)
    for l in range(own):
        core_copies.append(remote(
            part.at[l, half_rows(other)], part_core.at[l], pc_s.at[l], pc_r.at[l], width=other))
    x_copies = []
    for l in range(own):
        core_copies[l].wait_recv()
        part[l, my_half, :] = part[l, my_half, :] + part_core[l]
        for d in range(1, n_t):
            x_copies.append(remote(
                part.at[l, chunk_rows(x_peer(d), w)], part_x.at[l, d - 1],
                px_s.at[l, d - 1], px_r.at[l, d - 1], token=x_peer(d)))

    loads["topk"].wait()
    loads["offset"].wait()
    span = picked.shape[1]
    first_row = w * half + t * chunk
    start = first_row // span * span
    mask_rows = pl.ds(pl.multiple_of(first_row - start, chunk), chunk)
    for l in range(own):
        ids = topk[l, :, pl.ds(pl.multiple_of(start, span), span)]
        names = lax.broadcasted_iota(jnp.int32, (latents, span), 0)
        hit = jnp.zeros((latents, span), F32)
        for k in range(topk.shape[1]):
            hit = jnp.where(ids[k : k + 1, :] == names, 1.0, hit)
        picked[l] = hit.T

    high_target = table[1, 0]
    for p in range(1, pairs):
        high_target = jnp.maximum(high_target, table[1, p])
    for p in range(pairs):
        slot_of[p] = (table[1, p] == high_target).astype(jnp.int32)

    @pl.loop(0, layers)
    def _(l):
        high = jnp.int32(pairs)
        low = jnp.int32(pairs)
        for p in range(pairs):
            same = table[0, p] == l
            up = table[1, p] == high_target
            high = jnp.where(jnp.logical_and(same, up), p, high)
            low = jnp.where(jnp.logical_and(same, jnp.logical_not(up)), p, low)
        high_pair[l] = high
        low_pair[l] = low

    for l in range(own):
        pre = part[l, my_rows, :] + offset[pl.ds(l, 1), :]
        for d in range(1, n_t):
            x_copies[l * (n_t - 1) + d - 1].wait_recv()
            pre = pre + part_x[l, d - 1]
        preact[l] = pre
        soft = jnp.maximum(pre, 0.0) + jnp.log1p(jnp.exp(-jnp.abs(pre)))
        lat[z * own + l, my_rows, :] = (picked[l, mask_rows, :] * soft).astype(BF16)

    z_copies = [None]
    for d in range(1, n_z):
        here = lat.at[z_layers(z), my_rows]
        z_copies.append(remote(here, here, lz_s.at[d - 1], lz_r.at[d - 1], layer=z_peer(d)))
    x_copies = []
    for j in range(n_z):
        if j == 1:
            source_t[0] = source[0].T
        if j:
            z_copies[j].wait_recv()
        for d in range(1, n_t):
            here = lat.at[z_layers(z_from(j)), my_rows]
            x_copies.append(remote(
                here, here, lx_s.at[j, d - 1], lx_r.at[j, d - 1], token=x_peer(d)))
    for l in range(1, own):
        source_t[l] = source[l].T
    loads["decw"].wait()
    decw[pairs] = jnp.zeros((latents, width), BF16)
    core_copies = []
    for j in range(n_z):
        for d in range(1, n_t):
            x_copies[j * (n_t - 1) + d - 1].wait_recv()
        here = lat.at[z_layers(z_from(j)), my_half]
        core_copies.append(remote(here, here, lc_s.at[j], lc_r.at[j], width=other))
    loads["target"].wait()

    tile = 256
    lows = layers // 2

    def decode(rows):
        @pl.loop(0, width // tile)
        def _(n):
            cols = pl.ds(pl.multiple_of(n * tile, tile), tile)
            for slot, count, pair_of in ((1, layers, high_pair), (0, lows, low_pair)):
                acts = jnp.concatenate([lat[l, rows, :] for l in range(count)], axis=1)
                weight = jnp.concatenate([decw[pair_of[l], :, cols] for l in range(count)], axis=0)
                rebuilt = jnp.dot(acts, weight, preferred_element_type=F32)
                goal = target[slot, rows, cols].astype(F32)
                err[slot, rows, cols] = ((rebuilt - goal) * grad_scale).astype(BF16)

    decode(my_half)
    for j in range(n_z):
        core_copies[j].wait_recv()
    decode(half_rows(other))

    order = list(range(1, n_z)) + [0]
    core_copies = {}
    x_copies = {}
    z_copies = {}

    def spread_to(j):
        zz = z_peer(j)
        weight = jnp.concatenate(
            [
                jnp.concatenate([decw[high_pair[zz * own + i]], decw[low_pair[zz * own + i]]], axis=1)
                for i in range(own)
            ],
            axis=0,
        )
        both = jnp.concatenate([err[1], err[0]], axis=1)
        spread = lax.dot_general(
            both, weight, (((1,), (1,)), ((), ())), preferred_element_type=F32)
        for i in range(own):
            back[j, i] = spread[:, i * latents : (i + 1) * latents]
        core_copies[j] = remote(
            back.at[j, :, half_rows(other)], back_core.at[j], bc_s.at[j], bc_r.at[j], width=other)

    def send_x(j):
        core_copies[j].wait_recv()
        total = back[j, :, my_half, :] + back_core[j]
        back[j, :, my_half, :] = total
        back_xs[j] = total.astype(BF16)
        for d in range(1, n_t):
            rows = pl.ds(pl.multiple_of(x_peer(d) * chunk, chunk), chunk)
            x_copies[j, d] = remote(
                back_xs.at[j, :, rows], back_x.at[j, d - 1],
                bx_s.at[j, d - 1], bx_r.at[j, d - 1], token=x_peer(d))

    def send_z(j):
        total = back[j, :, my_rows, :]
        for d in range(1, n_t):
            x_copies[j, d].wait_recv()
            total = total + back_x[j, d - 1].astype(F32)
        if j:
            back_zs[j - 1] = total.astype(BF16)
            z_copies[j] = remote(
                back_zs.at[j - 1], back_z.at[j - 1], bz_s.at[j - 1], bz_r.at[j - 1], layer=z_peer(j))
        return total

    def dec_gradient(first, last):
        @pl.loop(first, last)
        def _(p):
            acts = lat[table[0, p]].T
            grad = jnp.dot(acts, err[slot_of[p]], preferred_element_type=F32)
            dec_out[p] = grad.astype(BF16)
            pltpu.make_async_copy(dec_out.at[p], decgrad_hbm.at[p], out_sem.at[p]).start()

    spread_to(order[0])
    for step in range(1, n_z):
        spread_to(order[step])
        send_x(order[step - 1])
    send_x(order[-1])
    for step in range(n_z):
        dec_gradient(step * pairs // n_z, (step + 1) * pairs // n_z)
        mine = send_z(order[step])
    for j in range(1, n_z):
        z_copies[j].wait_recv()
        mine = mine + back_z[j - 1].astype(F32)
    for l in range(own):
        pre_grad[l, my_rows, :] = (mine[l] * picked[l, mask_rows, :] * jax.nn.sigmoid(preact[l])).astype(BF16)

    here = pre_grad.at[:, my_rows]
    x_copies = [
        remote(here, here, gx_s.at[d - 1], gx_r.at[d - 1], token=x_peer(d)) for d in range(1, n_t)
    ]
    for copy in x_copies:
        copy.wait_recv()
    here = pre_grad.at[:, my_half]
    core_copy = remote(here, here, gc_s.at[0], gc_r.at[0], width=other)
    for l in range(own):
        enc_out[l] = jnp.dot(
            source_t[l, :, my_half], pre_grad[l, my_half, :], preferred_element_type=F32)
    core_copy.wait_recv()
    rest = half_rows(other)
    for l in range(own):
        enc_out[l] = enc_out[l] + jnp.dot(
            source_t[l, :, rest], pre_grad[l, rest, :], preferred_element_type=F32)
        pltpu.make_async_copy(enc_out.at[l], encgrad_hbm.at[l], out_sem.at[pairs + l]).start()
    for copy in sends:
        copy.wait_send()

    @pl.loop(0, pairs)
    def _(p):
        pltpu.make_async_copy(dec_out.at[p], decgrad_hbm.at[p], out_sem.at[p]).wait()

    for l in range(own):
        pltpu.make_async_copy(enc_out.at[l], encgrad_hbm.at[l], out_sem.at[pairs + l]).wait()


def shards(n_z, n_t, source_acts, enc_weight, enc_offset, topk_latents, pair_table, dec_weight, target_acts):
    own, tokens, width = source_acts.shape
    latents = enc_weight.shape[2]
    pairs = pair_table.shape[0]
    topk = topk_latents.shape[2]
    layers = own * n_z
    half = tokens // 2
    chunk = half // n_t
    peers = max(n_t - 1, 1)
    others = max(n_z - 1, 1)
    dims = (layers, n_z, n_t, own, tokens, width, latents, pairs)
    dma = pltpu.SemaphoreType.DMA
    scratch = [
        pltpu.VMEM((own, tokens, width), BF16),
        pltpu.VMEM((own, width, tokens), BF16),
        pltpu.VMEM((own, width, latents), BF16),
        pltpu.VMEM((own, latents), F32),
        pltpu.VMEM((own, topk, tokens), jnp.int32),
        pltpu.VMEM((pairs + 1, latents, width), BF16),
        pltpu.VMEM((2, tokens, width), BF16),
        pltpu.VMEM((own, tokens, latents), F32),
        pltpu.VMEM((own, half, latents), F32),
        pltpu.VMEM((own, peers, chunk, latents), F32),
        pltpu.VMEM((own, chunk, latents), F32),
        pltpu.VMEM((own, max(chunk, 128), latents), F32),
        pltpu.VMEM((layers, tokens, latents), BF16),
        pltpu.VMEM((2, tokens, width), BF16),
        pltpu.VMEM((n_z, own, tokens, latents), F32),
        pltpu.VMEM((n_z, own, half, latents), F32),
        pltpu.VMEM((n_z, own, half, latents), BF16),
        pltpu.VMEM((n_z, peers, own, chunk, latents), BF16),
        pltpu.VMEM((others, own, chunk, latents), BF16),
        pltpu.VMEM((others, own, chunk, latents), BF16),
        pltpu.VMEM((own, tokens, latents), BF16),
        pltpu.VMEM((pairs, latents, width), BF16),
        pltpu.VMEM((own, width, latents), F32),
        pltpu.SMEM((layers,), jnp.int32),
        pltpu.SMEM((layers,), jnp.int32),
        pltpu.SMEM((pairs,), jnp.int32),
        dma((2 * own + 4,)),
        dma((pairs + own,)),
    ]
    for shape in (
        (own,), (own, peers), (others,), (n_z, peers), (n_z,),
        (n_z,), (n_z, peers), (others,), (peers,), (1,),
    ):
        scratch += [dma(shape), dma(shape)]
    hbm = pl.BlockSpec(memory_space=pl.ANY)
    grads = pl.pallas_call(
        functools.partial(kernel, dims),
        out_shape=(
            jax.ShapeDtypeStruct((pairs, latents, width), BF16),
            jax.ShapeDtypeStruct((own, width, latents), F32),
        ),
        in_specs=[hbm, hbm, hbm, hbm, pl.BlockSpec(memory_space=pltpu.SMEM), hbm, hbm],
        out_specs=(hbm, hbm),
        scratch_shapes=scratch,
        compiler_params=pltpu.CompilerParams(
            collective_id=0, has_side_effects=True, vmem_limit_bytes=56 * 1024 * 1024
        ),
        cost_estimate=pl.CostEstimate(
            flops=2 * tokens * width * latents * (4 * pairs + 2 * own),
            bytes_accessed=2 * (2 * pairs * latents * width + 4 * tokens * width * own),
            transcendentals=0,
        ),
        name="transcoder_step",
    )(
        source_acts, enc_weight, enc_offset, jnp.swapaxes(topk_latents, 1, 2), pair_table.T,
        dec_weight, target_acts,
    )
    return write_out(*grads)


def write_kernel(dec_in, enc_in, dec_out, enc_out, sem):
    copies = [pltpu.make_async_copy(dec_in.at[p], dec_out.at[p], sem.at[p]) for p in range(dec_in.shape[0])]
    copies += [
        pltpu.make_async_copy(enc_in.at[l], enc_out.at[l], sem.at[len(copies) + l])
        for l in range(enc_in.shape[0])
    ]
    for copy in copies:
        copy.start()
    for copy in copies:
        copy.wait()


def write_out(dec, enc):
    hbm = pl.BlockSpec(memory_space=pl.ANY)
    return pl.pallas_call(
        write_kernel,
        out_shape=(
            jax.ShapeDtypeStruct(dec.shape, dec.dtype), jax.ShapeDtypeStruct(enc.shape, enc.dtype)
        ),
        in_specs=[hbm, hbm],
        out_specs=(hbm, hbm),
        scratch_shapes=[pltpu.SemaphoreType.DMA((dec.shape[0] + enc.shape[0],))],
        name="write_out",
    )(dec, enc)


def solution(mesh):
    in_specs = (
        P("layer", "groups", ("token", "width")),
        P("layer", ("token", "width"), None),
        P("layer", None),
        P("layer", "groups", None),
        P("layer", None),
        P("layer", None, ("token", "width")),
        P("layer", "groups", ("token", "width")),
    )
    out_specs = (
        P(("groups", "layer"), None, ("token", "width")),
        P(("groups", "layer"), ("token", "width"), None),
    )
    body = functools.partial(shards, mesh.shape["layer"], mesh.shape["token"])
    return jax.shard_map(body, mesh=mesh, in_specs=in_specs, out_specs=out_specs, check_vma=False)
```

```python
import functools

import jax
import jax.numpy as jnp
from jax import lax
from jax.experimental import pallas as pl
from jax.experimental.pallas import tpu as pltpu
from jax.sharding import PartitionSpec as P

grad_scale = 1.0 / 32.0
MESH = pl.DeviceIdType.MESH
F32 = jnp.float32
BF16 = jnp.bfloat16


def kernel(
    dims,
    source_hbm, encw_hbm, offset_hbm, topk_hbm, table, decw_hbm, target_hbm,
    decgrad_hbm, encgrad_hbm,
    source, source_t, encw, offset, topk, decw, target,
    part, part_core, part_x, preact, picked, lat, err,
    back, back_core, back_xs, back_x, back_zs, back_z, pre_grad, dec_out, enc_out,
    high_pair, low_pair, slot_of,
    in_sem, out_sem,
    pc_s, pc_r, px_s, px_r, lz_s, lz_r, lx_s, lx_r, lc_s, lc_r,
    bc_s, bc_r, bx_s, bx_r, bz_s, bz_r, gx_s, gx_r, gc_s, gc_r,
):
    layers, n_z, n_t, own, tokens, width, latents, pairs = dims
    half = tokens // 2
    chunk = half // n_t
    z = lax.axis_index("layer")
    t = lax.axis_index("token")
    w = lax.axis_index("width")
    other = 1 - w

    def half_rows(core):
        return pl.ds(pl.multiple_of(core * half, half), half)

    def chunk_rows(tok, core):
        return pl.ds(pl.multiple_of(core * half + tok * chunk, chunk), chunk)

    def x_peer(d):
        return lax.rem(t + d, n_t)

    def z_peer(d):
        return lax.rem(z + d, n_z)

    def z_from(d):
        return lax.rem(z - d + n_z, n_z)

    def z_layers(zz):
        return pl.ds(zz * own, own)

    my_half = half_rows(w)
    my_rows = chunk_rows(t, w)
    sends = []

    def remote(src, dst, ssem, rsem, **where):
        copy = pltpu.make_async_remote_copy(
            src_ref=src, dst_ref=dst, send_sem=ssem, recv_sem=rsem,
            device_id=where, device_id_type=MESH,
        )
        copy.start()
        sends.append(copy)
        return copy

    loads = {}

    def load(name, src, dst, sem):
        loads[name] = pltpu.make_async_copy(src, dst, in_sem.at[sem])
        loads[name].start()

    for l in range(own):
        load(("s", l), source_hbm.at[l], source.at[l], 2 * l)
        load(("e", l), encw_hbm.at[l], encw.at[l], 2 * l + 1)
    load("topk", topk_hbm, topk, 2 * own)
    load("offset", offset_hbm, offset, 2 * own + 1)
    load("decw", decw_hbm, decw.at[pl.ds(0, pairs)], 2 * own + 2)
    load("target", target_hbm, target, 2 * own + 3)

    barrier = pltpu.get_barrier_semaphore()
    pl.semaphore_signal(barrier, inc=1, device_id={"width": other}, device_id_type=MESH)
    for d in range(1, n_t):
        pl.semaphore_signal(barrier, inc=1, device_id={"token": x_peer(d)}, device_id_type=MESH)
    for d in range(1, n_z):
        pl.semaphore_signal(barrier, inc=1, device_id={"layer": z_peer(d)}, device_id_type=MESH)

    core_copies = []
    for l in range(own):
        loads[("s", l)].wait()
        loads[("e", l)].wait()
        part[l] = jnp.dot(source[l], encw[l], preferred_element_type=F32)
    pl.semaphore_wait(barrier, n_t + n_z - 1)
    for l in range(own):
        core_copies.append(remote(
            part.at[l, half_rows(other)], part_core.at[l], pc_s.at[l], pc_r.at[l], width=other))
    x_copies = []
    for l in range(own):
        core_copies[l].wait_recv()
        part[l, my_half, :] = part[l, my_half, :] + part_core[l]
        for d in range(1, n_t):
            x_copies.append(remote(
                part.at[l, chunk_rows(x_peer(d), w)], part_x.at[l, d - 1],
                px_s.at[l, d - 1], px_r.at[l, d - 1], token=x_peer(d)))

    loads["topk"].wait()
    loads["offset"].wait()
    span = picked.shape[1]
    first_row = w * half + t * chunk
    start = first_row // span * span
    mask_rows = pl.ds(pl.multiple_of(first_row - start, chunk), chunk)
    for l in range(own):
        ids = topk[l, :, pl.ds(pl.multiple_of(start, span), span)]
        names = lax.broadcasted_iota(jnp.int32, (latents, span), 0)
        hit = jnp.zeros((latents, span), F32)
        for k in range(topk.shape[1]):
            hit = jnp.where(ids[k : k + 1, :] == names, 1.0, hit)
        picked[l] = hit.T

    high_target = table[1, 0]
    for p in range(1, pairs):
        high_target = jnp.maximum(high_target, table[1, p])
    for p in range(pairs):
        slot_of[p] = (table[1, p] == high_target).astype(jnp.int32)

    @pl.loop(0, layers)
    def _(l):
        high = jnp.int32(pairs)
        low = jnp.int32(pairs)
        for p in range(pairs):
            same = table[0, p] == l
            up = table[1, p] == high_target
            high = jnp.where(jnp.logical_and(same, up), p, high)
            low = jnp.where(jnp.logical_and(same, jnp.logical_not(up)), p, low)
        high_pair[l] = high
        low_pair[l] = low

    for l in range(own):
        pre = part[l, my_rows, :] + offset[pl.ds(l, 1), :]
        for d in range(1, n_t):
            x_copies[l * (n_t - 1) + d - 1].wait_recv()
            pre = pre + part_x[l, d - 1]
        preact[l] = pre
        soft = jnp.maximum(pre, 0.0) + jnp.log1p(jnp.exp(-jnp.abs(pre)))
        lat[z * own + l, my_rows, :] = (picked[l, mask_rows, :] * soft).astype(BF16)

    z_copies = [None]
    for d in range(1, n_z):
        here = lat.at[z_layers(z), my_rows]
        z_copies.append(remote(here, here, lz_s.at[d - 1], lz_r.at[d - 1], layer=z_peer(d)))
    x_copies = []
    for j in range(n_z):
        if j == 1:
            source_t[0] = source[0].T
        if j:
            z_copies[j].wait_recv()
        for d in range(1, n_t):
            here = lat.at[z_layers(z_from(j)), my_rows]
            x_copies.append(remote(
                here, here, lx_s.at[j, d - 1], lx_r.at[j, d - 1], token=x_peer(d)))
    for l in range(1, own):
        source_t[l] = source[l].T
    loads["decw"].wait()
    decw[pairs] = jnp.zeros((latents, width), BF16)
    core_copies = []
    for j in range(n_z):
        for d in range(1, n_t):
            x_copies[j * (n_t - 1) + d - 1].wait_recv()
        here = lat.at[z_layers(z_from(j)), my_half]
        core_copies.append(remote(here, here, lc_s.at[j], lc_r.at[j], width=other))
    loads["target"].wait()

    tile = 256
    lows = layers // 2

    def decode(rows):
        @pl.loop(0, width // tile)
        def _(n):
            cols = pl.ds(pl.multiple_of(n * tile, tile), tile)
            for slot, count, pair_of in ((1, layers, high_pair), (0, lows, low_pair)):
                acts = jnp.concatenate([lat[l, rows, :] for l in range(count)], axis=1)
                weight = jnp.concatenate([decw[pair_of[l], :, cols] for l in range(count)], axis=0)
                rebuilt = jnp.dot(acts, weight, preferred_element_type=F32)
                goal = target[slot, rows, cols].astype(F32)
                err[slot, rows, cols] = ((rebuilt - goal) * grad_scale).astype(BF16)

    decode(my_half)
    for j in range(n_z):
        core_copies[j].wait_recv()
    decode(half_rows(other))

    order = list(range(1, n_z)) + [0]
    core_copies = {}
    x_copies = {}
    z_copies = {}

    def spread_to(j):
        zz = z_peer(j)
        weight = jnp.concatenate(
            [
                jnp.concatenate([decw[high_pair[zz * own + i]], decw[low_pair[zz * own + i]]], axis=1)
                for i in range(own)
            ],
            axis=0,
        )
        both = jnp.concatenate([err[1], err[0]], axis=1)
        spread = lax.dot_general(
            both, weight, (((1,), (1,)), ((), ())), preferred_element_type=F32)
        for i in range(own):
            back[j, i] = spread[:, i * latents : (i + 1) * latents]
        core_copies[j] = remote(
            back.at[j, :, half_rows(other)], back_core.at[j], bc_s.at[j], bc_r.at[j], width=other)

    def send_x(j):
        core_copies[j].wait_recv()
        total = back[j, :, my_half, :] + back_core[j]
        back[j, :, my_half, :] = total
        back_xs[j] = total.astype(BF16)
        for d in range(1, n_t):
            rows = pl.ds(pl.multiple_of(x_peer(d) * chunk, chunk), chunk)
            x_copies[j, d] = remote(
                back_xs.at[j, :, rows], back_x.at[j, d - 1],
                bx_s.at[j, d - 1], bx_r.at[j, d - 1], token=x_peer(d))

    def send_z(j):
        total = back[j, :, my_rows, :]
        for d in range(1, n_t):
            x_copies[j, d].wait_recv()
            total = total + back_x[j, d - 1].astype(F32)
        if j:
            back_zs[j - 1] = total.astype(BF16)
            z_copies[j] = remote(
                back_zs.at[j - 1], back_z.at[j - 1], bz_s.at[j - 1], bz_r.at[j - 1], layer=z_peer(j))
        return total

    def dec_gradient(first, last):
        @pl.loop(first, last)
        def _(p):
            acts = lat[table[0, p]].T
            grad = jnp.dot(acts, err[slot_of[p]], preferred_element_type=F32)
            dec_out[p] = grad.astype(BF16)
            pltpu.make_async_copy(dec_out.at[p], decgrad_hbm.at[p], out_sem.at[p]).start()

    spread_to(order[0])
    for step in range(1, n_z):
        spread_to(order[step])
        send_x(order[step - 1])
    send_x(order[-1])
    for step in range(n_z):
        dec_gradient(step * pairs // n_z, (step + 1) * pairs // n_z)
        mine = send_z(order[step])
    for j in range(1, n_z):
        z_copies[j].wait_recv()
        mine = mine + back_z[j - 1].astype(F32)
    for l in range(own):
        pre_grad[l, my_rows, :] = (mine[l] * picked[l, mask_rows, :] * jax.nn.sigmoid(preact[l])).astype(BF16)

    here = pre_grad.at[:, my_rows]
    x_copies = [
        remote(here, here, gx_s.at[d - 1], gx_r.at[d - 1], token=x_peer(d)) for d in range(1, n_t)
    ]
    for copy in x_copies:
        copy.wait_recv()
    here = pre_grad.at[:, my_half]
    core_copy = remote(here, here, gc_s.at[0], gc_r.at[0], width=other)
    for l in range(own):
        enc_out[l] = jnp.dot(
            source_t[l, :, my_half], pre_grad[l, my_half, :], preferred_element_type=F32)
    core_copy.wait_recv()
    rest = half_rows(other)
    for l in range(own):
        enc_out[l] = enc_out[l] + jnp.dot(
            source_t[l, :, rest], pre_grad[l, rest, :], preferred_element_type=F32)
        pltpu.make_async_copy(enc_out.at[l], encgrad_hbm.at[l], out_sem.at[pairs + l]).start()
    for copy in sends:
        copy.wait_send()

    @pl.loop(0, pairs)
    def _(p):
        pltpu.make_async_copy(dec_out.at[p], decgrad_hbm.at[p], out_sem.at[p]).wait()

    for l in range(own):
        pltpu.make_async_copy(enc_out.at[l], encgrad_hbm.at[l], out_sem.at[pairs + l]).wait()


def shards(n_z, n_t, source_acts, enc_weight, enc_offset, topk_latents, pair_table, dec_weight, target_acts):
    own, tokens, width = source_acts.shape
    latents = enc_weight.shape[2]
    pairs = pair_table.shape[0]
    topk = topk_latents.shape[2]
    layers = own * n_z
    half = tokens // 2
    chunk = half // n_t
    peers = max(n_t - 1, 1)
    others = max(n_z - 1, 1)
    dims = (layers, n_z, n_t, own, tokens, width, latents, pairs)
    dma = pltpu.SemaphoreType.DMA
    scratch = [
        pltpu.VMEM((own, tokens, width), BF16),
        pltpu.VMEM((own, width, tokens), BF16),
        pltpu.VMEM((own, width, latents), BF16),
        pltpu.VMEM((own, latents), F32),
        pltpu.VMEM((own, topk, tokens), jnp.int32),
        pltpu.VMEM((pairs + 1, latents, width), BF16),
        pltpu.VMEM((2, tokens, width), BF16),
        pltpu.VMEM((own, tokens, latents), F32),
        pltpu.VMEM((own, half, latents), F32),
        pltpu.VMEM((own, peers, chunk, latents), F32),
        pltpu.VMEM((own, chunk, latents), F32),
        pltpu.VMEM((own, max(chunk, 128), latents), F32),
        pltpu.VMEM((layers, tokens, latents), BF16),
        pltpu.VMEM((2, tokens, width), BF16),
        pltpu.VMEM((n_z, own, tokens, latents), F32),
        pltpu.VMEM((n_z, own, half, latents), F32),
        pltpu.VMEM((n_z, own, half, latents), BF16),
        pltpu.VMEM((n_z, peers, own, chunk, latents), BF16),
        pltpu.VMEM((others, own, chunk, latents), BF16),
        pltpu.VMEM((others, own, chunk, latents), BF16),
        pltpu.VMEM((own, tokens, latents), BF16),
        pltpu.VMEM((pairs, latents, width), BF16),
        pltpu.VMEM((own, width, latents), F32),
        pltpu.SMEM((layers,), jnp.int32),
        pltpu.SMEM((layers,), jnp.int32),
        pltpu.SMEM((pairs,), jnp.int32),
        dma((2 * own + 4,)),
        dma((pairs + own,)),
    ]
    for shape in (
        (own,), (own, peers), (others,), (n_z, peers), (n_z,),
        (n_z,), (n_z, peers), (others,), (peers,), (1,),
    ):
        scratch += [dma(shape), dma(shape)]
    hbm = pl.BlockSpec(memory_space=pl.ANY)
    grads = pl.pallas_call(
        functools.partial(kernel, dims),
        out_shape=(
            jax.ShapeDtypeStruct((pairs, latents, width), BF16),
            jax.ShapeDtypeStruct((own, width, latents), F32),
        ),
        in_specs=[hbm, hbm, hbm, hbm, pl.BlockSpec(memory_space=pltpu.SMEM), hbm, hbm],
        out_specs=(hbm, hbm),
        scratch_shapes=scratch,
        compiler_params=pltpu.CompilerParams(
            collective_id=0, has_side_effects=True, vmem_limit_bytes=56 * 1024 * 1024
        ),
        cost_estimate=pl.CostEstimate(
            flops=2 * tokens * width * latents * (4 * pairs + 2 * own),
            bytes_accessed=2 * (2 * pairs * latents * width + 4 * tokens * width * own),
            transcendentals=0,
        ),
        name="transcoder_step",
    )(
        source_acts, enc_weight, enc_offset, jnp.swapaxes(topk_latents, 1, 2), pair_table.T,
        dec_weight, target_acts,
    )
    return write_out(*grads)


def write_kernel(dec_in, enc_in, dec_out, enc_out, dec, enc, in_sem, out_sem):
    pairs, own = dec.shape[0], enc.shape[0]
    moves = [(dec_in.at[p], dec.at[p], dec_out.at[p]) for p in range(pairs)]
    moves += [(enc_in.at[l], enc.at[l], enc_out.at[l]) for l in range(own)]
    loads = [pltpu.make_async_copy(a, b, in_sem.at[i]) for i, (a, b, _) in enumerate(moves)]
    stores = [pltpu.make_async_copy(b, c, out_sem.at[i]) for i, (_, b, c) in enumerate(moves)]
    for load in loads:
        load.start()
    for load, store in zip(loads, stores):
        load.wait()
        store.start()
    for store in stores:
        store.wait()


def write_out(dec, enc):
    hbm = pl.BlockSpec(memory_space=pl.ANY)
    return pl.pallas_call(
        write_kernel,
        out_shape=(
            jax.ShapeDtypeStruct(dec.shape, dec.dtype), jax.ShapeDtypeStruct(enc.shape, enc.dtype)
        ),
        in_specs=[hbm, hbm],
        out_specs=(hbm, hbm),
        scratch_shapes=[
            pltpu.VMEM(dec.shape, dec.dtype),
            pltpu.VMEM(enc.shape, enc.dtype),
            pltpu.SemaphoreType.DMA((dec.shape[0] + enc.shape[0],)),
            pltpu.SemaphoreType.DMA((dec.shape[0] + enc.shape[0],)),
        ],
        compiler_params=pltpu.CompilerParams(vmem_limit_bytes=56 * 1024 * 1024),
        name="write_out",
    )(dec, enc)


def solution(mesh):
    in_specs = (
        P("layer", "groups", ("token", "width")),
        P("layer", ("token", "width"), None),
        P("layer", None),
        P("layer", "groups", None),
        P("layer", None),
        P("layer", None, ("token", "width")),
        P("layer", "groups", ("token", "width")),
    )
    out_specs = (
        P(("groups", "layer"), None, ("token", "width")),
        P(("groups", "layer"), ("token", "width"), None),
    )
    body = functools.partial(shards, mesh.shape["layer"], mesh.shape["token"])
    return jax.shard_map(body, mesh=mesh, in_specs=in_specs, out_specs=out_specs, check_vma=False)
```

```python
import functools

import jax
import jax.numpy as jnp
from jax import lax
from jax.experimental import pallas as pl
from jax.experimental.pallas import tpu as pltpu
from jax.sharding import PartitionSpec as P

grad_scale = 1.0 / 32.0
MESH = pl.DeviceIdType.MESH
F32 = jnp.float32
BF16 = jnp.bfloat16


def kernel(
    dims,
    source_hbm, encw_hbm, offset_hbm, topk_hbm, table, decw_hbm, target_hbm,
    decgrad_hbm, encgrad_hbm,
    source, source_t, encw, offset, topk, decw, target,
    part, part_core, part_x, preact, picked, lat, err,
    back, back_core, back_xs, back_x, back_zs, back_z, pre_grad, dec_out, enc_out,
    high_pair, low_pair, slot_of,
    in_sem, out_sem,
    pc_s, pc_r, px_s, px_r, lz_s, lz_r, lx_s, lx_r, lc_s, lc_r,
    bc_s, bc_r, bx_s, bx_r, bz_s, bz_r, gx_s, gx_r, gc_s, gc_r,
):
    layers, n_z, n_t, own, tokens, width, latents, pairs = dims
    half = tokens // 2
    chunk = half // n_t
    z = lax.axis_index("layer")
    t = lax.axis_index("token")
    w = lax.axis_index("width")
    other = 1 - w

    def half_rows(core):
        return pl.ds(pl.multiple_of(core * half, half), half)

    def chunk_rows(tok, core):
        return pl.ds(pl.multiple_of(core * half + tok * chunk, chunk), chunk)

    def x_peer(d):
        return lax.rem(t + d, n_t)

    def z_peer(d):
        return lax.rem(z + d, n_z)

    def z_from(d):
        return lax.rem(z - d + n_z, n_z)

    def z_layers(zz):
        return pl.ds(zz * own, own)

    my_half = half_rows(w)
    my_rows = chunk_rows(t, w)
    sends = []

    def remote(src, dst, ssem, rsem, **where):
        copy = pltpu.make_async_remote_copy(
            src_ref=src, dst_ref=dst, send_sem=ssem, recv_sem=rsem,
            device_id=where, device_id_type=MESH,
        )
        copy.start()
        sends.append(copy)
        return copy

    loads = {}

    def load(name, src, dst, sem):
        loads[name] = pltpu.make_async_copy(src, dst, in_sem.at[sem])
        loads[name].start()

    for l in range(own):
        load(("s", l), source_hbm.at[l], source.at[l], 2 * l)
        load(("e", l), encw_hbm.at[l], encw.at[l], 2 * l + 1)
    load("topk", topk_hbm, topk, 2 * own)
    load("offset", offset_hbm, offset, 2 * own + 1)
    load("decw", decw_hbm, decw.at[pl.ds(0, pairs)], 2 * own + 2)
    load("target", target_hbm, target, 2 * own + 3)

    barrier = pltpu.get_barrier_semaphore()
    pl.semaphore_signal(barrier, inc=1, device_id={"width": other}, device_id_type=MESH)
    for d in range(1, n_t):
        pl.semaphore_signal(barrier, inc=1, device_id={"token": x_peer(d)}, device_id_type=MESH)
    for d in range(1, n_z):
        pl.semaphore_signal(barrier, inc=1, device_id={"layer": z_peer(d)}, device_id_type=MESH)

    core_copies = []
    for l in range(own):
        loads[("s", l)].wait()
        loads[("e", l)].wait()
        part[l] = jnp.dot(source[l], encw[l], preferred_element_type=F32)
    pl.semaphore_wait(barrier, n_t + n_z - 1)
    for l in range(own):
        core_copies.append(remote(
            part.at[l, half_rows(other)], part_core.at[l], pc_s.at[l], pc_r.at[l], width=other))
    first_copies = []
    for l in range(own):
        core_copies[l].wait_recv()
        part[l, my_half, :] = part[l, my_half, :] + part_core[l]
        for d in range(1, n_t):
            first_copies.append(remote(
                part.at[l, chunk_rows(x_peer(d), w)], part_x.at[l, d - 1],
                px_s.at[l, d - 1], px_r.at[l, d - 1], token=x_peer(d)))

    loads["topk"].wait()
    loads["offset"].wait()
    span = picked.shape[1]
    first_row = w * half + t * chunk
    start = first_row // span * span
    mask_rows = pl.ds(pl.multiple_of(first_row - start, chunk), chunk)
    for l in range(own):
        ids = topk[l, :, pl.ds(pl.multiple_of(start, span), span)]
        names = lax.broadcasted_iota(jnp.int32, (latents, span), 0)
        hit = jnp.zeros((latents, span), F32)
        for k in range(topk.shape[1]):
            hit = jnp.where(ids[k : k + 1, :] == names, 1.0, hit)
        picked[l] = hit.T

    high_target = table[1, 0]
    for p in range(1, pairs):
        high_target = jnp.maximum(high_target, table[1, p])
    for p in range(pairs):
        slot_of[p] = (table[1, p] == high_target).astype(jnp.int32)

    @pl.loop(0, layers)
    def _(l):
        high = jnp.int32(pairs)
        low = jnp.int32(pairs)
        for p in range(pairs):
            same = table[0, p] == l
            up = table[1, p] == high_target
            high = jnp.where(jnp.logical_and(same, up), p, high)
            low = jnp.where(jnp.logical_and(same, jnp.logical_not(up)), p, low)
        high_pair[l] = high
        low_pair[l] = low

    z_copies = {}
    x_copies = {}

    def pass_x(j, l):
        for d in range(1, n_t):
            here = lat.at[z_from(j) * own + l, my_rows]
            x_copies[j, l, d] = remote(
                here, here, lx_s.at[j, l, d - 1], lx_r.at[j, l, d - 1], token=x_peer(d))

    for l in range(own):
        pre = part[l, my_rows, :] + offset[pl.ds(l, 1), :]
        for d in range(1, n_t):
            first_copies[l * (n_t - 1) + d - 1].wait_recv()
            pre = pre + part_x[l, d - 1]
        preact[l] = pre
        soft = jnp.maximum(pre, 0.0) + jnp.log1p(jnp.exp(-jnp.abs(pre)))
        lat[z * own + l, my_rows, :] = (picked[l, mask_rows, :] * soft).astype(BF16)

        for d in range(1, n_z):
            here = lat.at[z * own + l, my_rows]
            z_copies[d, l] = remote(
                here, here, lz_s.at[d - 1, l], lz_r.at[d - 1, l], layer=z_peer(d))
        pass_x(0, l)
    source_t[0] = source[0].T
    for j in range(1, n_z):
        for l in range(own):
            z_copies[j, l].wait_recv()
            pass_x(j, l)
    for l in range(1, own):
        source_t[l] = source[l].T
    loads["decw"].wait()
    decw[pairs] = jnp.zeros((latents, width), BF16)
    core_copies = []
    for j in range(n_z):
        for l in range(own):
            for d in range(1, n_t):
                x_copies[j, l, d].wait_recv()
        here = lat.at[z_layers(z_from(j)), my_half]
        core_copies.append(remote(here, here, lc_s.at[j], lc_r.at[j], width=other))
    loads["target"].wait()

    tile = 256
    lows = layers // 2

    def decode(rows):
        @pl.loop(0, width // tile)
        def _(n):
            cols = pl.ds(pl.multiple_of(n * tile, tile), tile)
            for slot, count, pair_of in ((1, layers, high_pair), (0, lows, low_pair)):
                acts = jnp.concatenate([lat[l, rows, :] for l in range(count)], axis=1)
                weight = jnp.concatenate([decw[pair_of[l], :, cols] for l in range(count)], axis=0)
                rebuilt = jnp.dot(acts, weight, preferred_element_type=F32)
                goal = target[slot, rows, cols].astype(F32)
                err[slot, rows, cols] = ((rebuilt - goal) * grad_scale).astype(BF16)

    decode(my_half)
    for j in range(n_z):
        core_copies[j].wait_recv()
    decode(half_rows(other))

    order = list(range(1, n_z)) + [0]
    core_copies = {}
    x_copies = {}
    z_copies = {}

    def spread_to(j):
        zz = z_peer(j)
        def times(slot, pair_of):
            weight = jnp.concatenate([decw[pair_of[zz * own + i]] for i in range(own)], axis=0)
            return lax.dot_general(
                err[slot], weight, (((1,), (1,)), ((), ())), preferred_element_type=F32)

        spread = times(1, high_pair)
        for i in range(own):
            back[j, i] = spread[:, i * latents : (i + 1) * latents]

        @pl.when(zz * own < lows)
        def _():
            spread = times(0, low_pair)
            for i in range(own):
                back[j, i] = back[j, i] + spread[:, i * latents : (i + 1) * latents]

        core_copies[j] = remote(
            back.at[j, :, half_rows(other)], back_core.at[j], bc_s.at[j], bc_r.at[j], width=other)

    def send_x(j):
        core_copies[j].wait_recv()
        total = back[j, :, my_half, :] + back_core[j]
        back[j, :, my_half, :] = total
        back_xs[j] = total.astype(BF16)
        for d in range(1, n_t):
            rows = pl.ds(pl.multiple_of(x_peer(d) * chunk, chunk), chunk)
            x_copies[j, d] = remote(
                back_xs.at[j, :, rows], back_x.at[j, d - 1],
                bx_s.at[j, d - 1], bx_r.at[j, d - 1], token=x_peer(d))

    def send_z(j):
        total = back[j, :, my_rows, :]
        for d in range(1, n_t):
            x_copies[j, d].wait_recv()
            total = total + back_x[j, d - 1].astype(F32)
        if j:
            back_zs[j - 1] = total.astype(BF16)
            z_copies[j] = remote(
                back_zs.at[j - 1], back_z.at[j - 1], bz_s.at[j - 1], bz_r.at[j - 1], layer=z_peer(j))
        return total

    def dec_gradient(first, last):
        @pl.loop(first, last)
        def _(p):
            acts = lat[table[0, p]].T
            grad = jnp.dot(acts, err[slot_of[p]], preferred_element_type=F32)
            dec_out[p] = grad.astype(BF16)
            pltpu.make_async_copy(dec_out.at[p], decgrad_hbm.at[p], out_sem.at[p]).start()

    spread_to(order[0])
    for step in range(1, n_z):
        spread_to(order[step])
        send_x(order[step - 1])
    send_x(order[-1])
    for step in range(n_z):
        mine = send_z(order[step])
        dec_gradient(step * pairs // n_z, (step + 1) * pairs // n_z)
    for j in range(1, n_z):
        z_copies[j].wait_recv()
        mine = mine + back_z[j - 1].astype(F32)
    for l in range(own):
        pre_grad[l, my_rows, :] = (mine[l] * picked[l, mask_rows, :] * jax.nn.sigmoid(preact[l])).astype(BF16)

    here = pre_grad.at[:, my_rows]
    x_copies = [
        remote(here, here, gx_s.at[d - 1], gx_r.at[d - 1], token=x_peer(d)) for d in range(1, n_t)
    ]
    for copy in x_copies:
        copy.wait_recv()
    here = pre_grad.at[:, my_half]
    core_copy = remote(here, here, gc_s.at[0], gc_r.at[0], width=other)
    for l in range(own):
        enc_out[l] = jnp.dot(
            source_t[l, :, my_half], pre_grad[l, my_half, :], preferred_element_type=F32)
    core_copy.wait_recv()
    rest = half_rows(other)
    for l in range(own):
        enc_out[l] = enc_out[l] + jnp.dot(
            source_t[l, :, rest], pre_grad[l, rest, :], preferred_element_type=F32)
        pltpu.make_async_copy(enc_out.at[l], encgrad_hbm.at[l], out_sem.at[pairs + l]).start()
    for copy in sends:
        copy.wait_send()

    @pl.loop(0, pairs)
    def _(p):
        pltpu.make_async_copy(dec_out.at[p], decgrad_hbm.at[p], out_sem.at[p]).wait()

    for l in range(own):
        pltpu.make_async_copy(enc_out.at[l], encgrad_hbm.at[l], out_sem.at[pairs + l]).wait()


def shards(n_z, n_t, source_acts, enc_weight, enc_offset, topk_latents, pair_table, dec_weight, target_acts):
    own, tokens, width = source_acts.shape
    latents = enc_weight.shape[2]
    pairs = pair_table.shape[0]
    topk = topk_latents.shape[2]
    layers = own * n_z
    half = tokens // 2
    chunk = half // n_t
    peers = max(n_t - 1, 1)
    others = max(n_z - 1, 1)
    dims = (layers, n_z, n_t, own, tokens, width, latents, pairs)
    dma = pltpu.SemaphoreType.DMA
    scratch = [
        pltpu.VMEM((own, tokens, width), BF16),
        pltpu.VMEM((own, width, tokens), BF16),
        pltpu.VMEM((own, width, latents), BF16),
        pltpu.VMEM((own, latents), F32),
        pltpu.VMEM((own, topk, tokens), jnp.int32),
        pltpu.VMEM((pairs + 1, latents, width), BF16),
        pltpu.VMEM((2, tokens, width), BF16),
        pltpu.VMEM((own, tokens, latents), F32),
        pltpu.VMEM((own, half, latents), F32),
        pltpu.VMEM((own, peers, chunk, latents), F32),
        pltpu.VMEM((own, chunk, latents), F32),
        pltpu.VMEM((own, max(chunk, 128), latents), F32),
        pltpu.VMEM((layers, tokens, latents), BF16),
        pltpu.VMEM((2, tokens, width), BF16),
        pltpu.VMEM((n_z, own, tokens, latents), F32),
        pltpu.VMEM((n_z, own, half, latents), F32),
        pltpu.VMEM((n_z, own, half, latents), BF16),
        pltpu.VMEM((n_z, peers, own, chunk, latents), BF16),
        pltpu.VMEM((others, own, chunk, latents), BF16),
        pltpu.VMEM((others, own, chunk, latents), BF16),
        pltpu.VMEM((own, tokens, latents), BF16),
        pltpu.VMEM((pairs, latents, width), BF16),
        pltpu.VMEM((own, width, latents), F32),
        pltpu.SMEM((layers,), jnp.int32),
        pltpu.SMEM((layers,), jnp.int32),
        pltpu.SMEM((pairs,), jnp.int32),
        dma((2 * own + 4,)),
        dma((pairs + own,)),
    ]
    for shape in (
        (own,), (own, peers), (others, own), (n_z, own, peers), (n_z,),
        (n_z,), (n_z, peers), (others,), (peers,), (1,),
    ):
        scratch += [dma(shape), dma(shape)]
    hbm = pl.BlockSpec(memory_space=pl.ANY)
    grads = pl.pallas_call(
        functools.partial(kernel, dims),
        out_shape=(
            jax.ShapeDtypeStruct((pairs, latents, width), BF16),
            jax.ShapeDtypeStruct((own, width, latents), F32),
        ),
        in_specs=[hbm, hbm, hbm, hbm, pl.BlockSpec(memory_space=pltpu.SMEM), hbm, hbm],
        out_specs=(hbm, hbm),
        scratch_shapes=scratch,
        compiler_params=pltpu.CompilerParams(
            collective_id=0, has_side_effects=True, vmem_limit_bytes=56 * 1024 * 1024
        ),
        cost_estimate=pl.CostEstimate(
            flops=2 * tokens * width * latents * (4 * pairs + 2 * own),
            bytes_accessed=2 * (2 * pairs * latents * width + 4 * tokens * width * own),
            transcendentals=0,
        ),
        name="transcoder_step",
    )(
        source_acts, enc_weight, enc_offset, jnp.swapaxes(topk_latents, 1, 2), pair_table.T,
        dec_weight, target_acts,
    )
    return write_out(*grads)


def write_kernel(dec_in, enc_in, dec_out, enc_out, dec, enc, in_sem, out_sem):
    pairs, own = dec.shape[0], enc.shape[0]
    moves = [(dec_in.at[p], dec.at[p], dec_out.at[p]) for p in range(pairs)]
    moves += [(enc_in.at[l], enc.at[l], enc_out.at[l]) for l in range(own)]
    loads = [pltpu.make_async_copy(a, b, in_sem.at[i]) for i, (a, b, _) in enumerate(moves)]
    stores = [pltpu.make_async_copy(b, c, out_sem.at[i]) for i, (_, b, c) in enumerate(moves)]
    for load in loads:
        load.start()
    for load, store in zip(loads, stores):
        load.wait()
        store.start()
    for store in stores:
        store.wait()


def write_out(dec, enc):
    hbm = pl.BlockSpec(memory_space=pl.ANY)
    return pl.pallas_call(
        write_kernel,
        out_shape=(
            jax.ShapeDtypeStruct(dec.shape, dec.dtype), jax.ShapeDtypeStruct(enc.shape, enc.dtype)
        ),
        in_specs=[hbm, hbm],
        out_specs=(hbm, hbm),
        scratch_shapes=[
            pltpu.VMEM(dec.shape, dec.dtype),
            pltpu.VMEM(enc.shape, enc.dtype),
            pltpu.SemaphoreType.DMA((dec.shape[0] + enc.shape[0],)),
            pltpu.SemaphoreType.DMA((dec.shape[0] + enc.shape[0],)),
        ],
        compiler_params=pltpu.CompilerParams(vmem_limit_bytes=56 * 1024 * 1024),
        name="write_out",
    )(dec, enc)


def solution(mesh):
    in_specs = (
        P("layer", "groups", ("token", "width")),
        P("layer", ("token", "width"), None),
        P("layer", None),
        P("layer", "groups", None),
        P("layer", None),
        P("layer", None, ("token", "width")),
        P("layer", "groups", ("token", "width")),
    )
    out_specs = (
        P(("groups", "layer"), None, ("token", "width")),
        P(("groups", "layer"), ("token", "width"), None),
    )
    body = functools.partial(shards, mesh.shape["layer"], mesh.shape["token"])
    return jax.shard_map(body, mesh=mesh, in_specs=in_specs, out_specs=out_specs, check_vma=False)
```

```python
import functools

import jax
import jax.numpy as jnp
from jax import lax
from jax.experimental import pallas as pl
from jax.experimental.pallas import tpu as pltpu
from jax.sharding import PartitionSpec as P

grad_scale = 1.0 / 32.0
MESH = pl.DeviceIdType.MESH
F32 = jnp.float32
BF16 = jnp.bfloat16


def kernel(
    dims,
    source_hbm, encw_hbm, offset_hbm, topk_hbm, table, decw_hbm, target_hbm,
    decgrad_hbm, encgrad_hbm,
    source, source_t, encw, offset, topk, decw, target,
    part, part_core, part_x, preact, picked, lat, err,
    back, back_core, back_xs, back_x, back_zs, back_z, pre_grad, dec_out, enc_out,
    high_pair, low_pair, slot_of,
    in_sem, out_sem,
    pc_s, pc_r, px_s, px_r, lz_s, lz_r, lx_s, lx_r, lc_s, lc_r,
    bc_s, bc_r, bx_s, bx_r, bz_s, bz_r, gx_s, gx_r, gc_s, gc_r,
):
    layers, n_z, n_t, own, tokens, width, latents, pairs = dims
    half = tokens // 2
    chunk = half // n_t
    z = lax.axis_index("layer")
    t = lax.axis_index("token")
    w = lax.axis_index("width")
    other = 1 - w

    def half_rows(core):
        return pl.ds(pl.multiple_of(core * half, half), half)

    def chunk_rows(tok, core):
        return pl.ds(pl.multiple_of(core * half + tok * chunk, chunk), chunk)

    def x_peer(d):
        return lax.rem(t + d, n_t)

    def z_peer(d):
        return lax.rem(z + d, n_z)

    def z_from(d):
        return lax.rem(z - d + n_z, n_z)

    def z_layers(zz):
        return pl.ds(zz * own, own)

    my_half = half_rows(w)
    my_rows = chunk_rows(t, w)
    sends = []

    def remote(src, dst, ssem, rsem, **where):
        copy = pltpu.make_async_remote_copy(
            src_ref=src, dst_ref=dst, send_sem=ssem, recv_sem=rsem,
            device_id=where, device_id_type=MESH,
        )
        copy.start()
        sends.append(copy)
        return copy

    loads = {}

    def load(name, src, dst, sem):
        loads[name] = pltpu.make_async_copy(src, dst, in_sem.at[sem])
        loads[name].start()

    for l in range(own):
        load(("s", l), source_hbm.at[l], source.at[l], 2 * l)
        load(("e", l), encw_hbm.at[l], encw.at[l], 2 * l + 1)
    load("topk", topk_hbm, topk, 2 * own)
    load("offset", offset_hbm, offset, 2 * own + 1)
    load("decw", decw_hbm, decw.at[pl.ds(0, pairs)], 2 * own + 2)
    load("target", target_hbm, target, 2 * own + 3)

    barrier = pltpu.get_barrier_semaphore()
    pl.semaphore_signal(barrier, inc=1, device_id={"width": other}, device_id_type=MESH)
    for d in range(1, n_t):
        pl.semaphore_signal(barrier, inc=1, device_id={"token": x_peer(d)}, device_id_type=MESH)
    for d in range(1, n_z):
        pl.semaphore_signal(barrier, inc=1, device_id={"layer": z_peer(d)}, device_id_type=MESH)

    core_copies = []
    for l in range(own):
        loads[("s", l)].wait()
        loads[("e", l)].wait()
        part[l] = jnp.dot(source[l], encw[l], preferred_element_type=F32)
    pl.semaphore_wait(barrier, n_t + n_z - 1)
    for l in range(own):
        core_copies.append(remote(
            part.at[l, half_rows(other)], part_core.at[l], pc_s.at[l], pc_r.at[l], width=other))
    first_copies = []
    for l in range(own):
        core_copies[l].wait_recv()
        part[l, my_half, :] = part[l, my_half, :] + part_core[l]
        for d in range(1, n_t):
            first_copies.append(remote(
                part.at[l, chunk_rows(x_peer(d), w)], part_x.at[l, d - 1],
                px_s.at[l, d - 1], px_r.at[l, d - 1], token=x_peer(d)))

    loads["topk"].wait()
    loads["offset"].wait()
    span = picked.shape[1]
    first_row = w * half + t * chunk
    start = first_row // span * span
    mask_rows = pl.ds(pl.multiple_of(first_row - start, chunk), chunk)
    for l in range(own):
        ids = topk[l, :, pl.ds(pl.multiple_of(start, span), span)]
        names = lax.broadcasted_iota(jnp.int32, (latents, span), 0)
        hit = jnp.zeros((latents, span), F32)
        for k in range(topk.shape[1]):
            hit = jnp.where(ids[k : k + 1, :] == names, 1.0, hit)
        picked[l] = hit.T

    high_target = table[1, 0]
    for p in range(1, pairs):
        high_target = jnp.maximum(high_target, table[1, p])
    for p in range(pairs):
        slot_of[p] = (table[1, p] == high_target).astype(jnp.int32)

    @pl.loop(0, layers)
    def _(l):
        high = jnp.int32(pairs)
        low = jnp.int32(pairs)
        for p in range(pairs):
            same = table[0, p] == l
            up = table[1, p] == high_target
            high = jnp.where(jnp.logical_and(same, up), p, high)
            low = jnp.where(jnp.logical_and(same, jnp.logical_not(up)), p, low)
        high_pair[l] = high
        low_pair[l] = low

    z_copies = {}
    x_copies = {}

    def pass_x(j, l):
        for d in range(1, n_t):
            here = lat.at[z_from(j) * own + l, my_rows]
            x_copies[j, l, d] = remote(
                here, here, lx_s.at[j, l, d - 1], lx_r.at[j, l, d - 1], token=x_peer(d))

    for l in range(own):
        pre = part[l, my_rows, :] + offset[pl.ds(l, 1), :]
        for d in range(1, n_t):
            first_copies[l * (n_t - 1) + d - 1].wait_recv()
            pre = pre + part_x[l, d - 1]
        preact[l] = pre
        soft = jnp.maximum(pre, 0.0) + jnp.log1p(jnp.exp(-jnp.abs(pre)))
        lat[z * own + l, my_rows, :] = (picked[l, mask_rows, :] * soft).astype(BF16)

        for d in range(1, n_z):
            here = lat.at[z * own + l, my_rows]
            z_copies[d, l] = remote(
                here, here, lz_s.at[d - 1, l], lz_r.at[d - 1, l], layer=z_peer(d))
        pass_x(0, l)
    source_t[0] = source[0].T
    for j in range(1, n_z):
        for l in range(own):
            z_copies[j, l].wait_recv()
            pass_x(j, l)
    for l in range(1, own):
        source_t[l] = source[l].T
    loads["decw"].wait()
    decw[pairs] = jnp.zeros((latents, width), BF16)
    core_copies = []
    for j in range(n_z):
        for l in range(own):
            for d in range(1, n_t):
                x_copies[j, l, d].wait_recv()
        here = lat.at[z_layers(z_from(j)), my_half]
        core_copies.append(remote(here, here, lc_s.at[j], lc_r.at[j], width=other))
    loads["target"].wait()

    tile = 256
    lows = layers // 2

    def decode(rows):
        @pl.loop(0, width // tile)
        def _(n):
            cols = pl.ds(pl.multiple_of(n * tile, tile), tile)
            for slot, count, pair_of in ((1, layers, high_pair), (0, lows, low_pair)):
                acts = jnp.concatenate([lat[l, rows, :] for l in range(count)], axis=1)
                weight = jnp.concatenate([decw[pair_of[l], :, cols] for l in range(count)], axis=0)
                rebuilt = jnp.dot(acts, weight, preferred_element_type=F32)
                goal = target[slot, rows, cols].astype(F32)
                err[slot, rows, cols] = ((rebuilt - goal) * grad_scale).astype(BF16)

    decode(my_half)
    for j in range(n_z):
        core_copies[j].wait_recv()
    decode(half_rows(other))

    order = list(range(1, n_z)) + [0]
    core_copies = {}
    x_copies = {}
    z_copies = {}

    def spread_to(j):
        zz = z_peer(j)
        def times(slot, pair_of, rows):
            weight = jnp.concatenate([decw[pair_of[zz * own + i]] for i in range(own)], axis=0)
            return lax.dot_general(
                err[slot, rows, :], weight, (((1,), (1,)), ((), ())), preferred_element_type=F32)

        def half_spread(rows):
            spread = times(1, high_pair, rows)
            for i in range(own):
                back[j, i, rows, :] = spread[:, i * latents : (i + 1) * latents]

            @pl.when(zz * own < lows)
            def _():
                spread = times(0, low_pair, rows)
                for i in range(own):
                    back[j, i, rows, :] = (
                        back[j, i, rows, :] + spread[:, i * latents : (i + 1) * latents])

        half_spread(half_rows(other))
        core_copies[j] = remote(
            back.at[j, :, half_rows(other)], back_core.at[j], bc_s.at[j], bc_r.at[j], width=other)
        half_spread(my_half)

    def send_x(j):
        core_copies[j].wait_recv()
        for i in range(own):
            total = back[j, i, my_half, :] + back_core[j, i]
            back[j, i, my_half, :] = total
            back_xs[j, i] = total.astype(BF16)
            for d in range(1, n_t):
                rows = pl.ds(pl.multiple_of(x_peer(d) * chunk, chunk), chunk)
                x_copies[j, i, d] = remote(
                    back_xs.at[j, i, rows], back_x.at[j, d - 1, i],
                    bx_s.at[j, d - 1, i], bx_r.at[j, d - 1, i], token=x_peer(d))

    def send_z(j):
        totals = []
        for i in range(own):
            total = back[j, i, my_rows, :]
            for d in range(1, n_t):
                x_copies[j, i, d].wait_recv()
                total = total + back_x[j, d - 1, i].astype(F32)
            totals.append(total)
            if j:
                back_zs[j - 1, i] = total.astype(BF16)
                z_copies[j, i] = remote(
                    back_zs.at[j - 1, i], back_z.at[j - 1, i],
                    bz_s.at[j - 1, i], bz_r.at[j - 1, i], layer=z_peer(j))
        return totals

    def dec_gradient(first, last):
        @pl.loop(first, last)
        def _(p):
            acts = lat[table[0, p]].T
            grad = jnp.dot(acts, err[slot_of[p]], preferred_element_type=F32)
            dec_out[p] = grad.astype(BF16)
            pltpu.make_async_copy(dec_out.at[p], decgrad_hbm.at[p], out_sem.at[p]).start()

    spread_to(order[0])
    for step in range(1, n_z):
        spread_to(order[step])
        send_x(order[step - 1])
    send_x(order[-1])
    for step in range(n_z):
        mine = send_z(order[step])
        dec_gradient(step * pairs // n_z, (step + 1) * pairs // n_z)
    g_copies = {}
    for l in range(own):
        grad = mine[l]
        for j in range(1, n_z):
            z_copies[j, l].wait_recv()
            grad = grad + back_z[j - 1, l].astype(F32)
        pre_grad[l, my_rows, :] = (
            grad * picked[l, mask_rows, :] * jax.nn.sigmoid(preact[l])).astype(BF16)
        here = pre_grad.at[l, my_rows]
        for d in range(1, n_t):
            g_copies[l, d] = remote(
                here, here, gx_s.at[d - 1, l], gx_r.at[d - 1, l], token=x_peer(d))
    core_copies = []
    for l in range(own):
        for d in range(1, n_t):
            g_copies[l, d].wait_recv()
        here = pre_grad.at[l, my_half]
        core_copies.append(remote(here, here, gc_s.at[l], gc_r.at[l], width=other))
    for l in range(own):
        enc_out[l] = jnp.dot(
            source_t[l, :, my_half], pre_grad[l, my_half, :], preferred_element_type=F32)
    rest = half_rows(other)
    for l in range(own):
        core_copies[l].wait_recv()
        enc_out[l] = enc_out[l] + jnp.dot(
            source_t[l, :, rest], pre_grad[l, rest, :], preferred_element_type=F32)
        pltpu.make_async_copy(enc_out.at[l], encgrad_hbm.at[l], out_sem.at[pairs + l]).start()
    for copy in sends:
        copy.wait_send()

    @pl.loop(0, pairs)
    def _(p):
        pltpu.make_async_copy(dec_out.at[p], decgrad_hbm.at[p], out_sem.at[p]).wait()

    for l in range(own):
        pltpu.make_async_copy(enc_out.at[l], encgrad_hbm.at[l], out_sem.at[pairs + l]).wait()


def shards(n_z, n_t, source_acts, enc_weight, enc_offset, topk_latents, pair_table, dec_weight, target_acts):
    own, tokens, width = source_acts.shape
    latents = enc_weight.shape[2]
    pairs = pair_table.shape[0]
    topk = topk_latents.shape[2]
    layers = own * n_z
    half = tokens // 2
    chunk = half // n_t
    peers = max(n_t - 1, 1)
    others = max(n_z - 1, 1)
    dims = (layers, n_z, n_t, own, tokens, width, latents, pairs)
    dma = pltpu.SemaphoreType.DMA
    scratch = [
        pltpu.VMEM((own, tokens, width), BF16),
        pltpu.VMEM((own, width, tokens), BF16),
        pltpu.VMEM((own, width, latents), BF16),
        pltpu.VMEM((own, latents), F32),
        pltpu.VMEM((own, topk, tokens), jnp.int32),
        pltpu.VMEM((pairs + 1, latents, width), BF16),
        pltpu.VMEM((2, tokens, width), BF16),
        pltpu.VMEM((own, tokens, latents), F32),
        pltpu.VMEM((own, half, latents), F32),
        pltpu.VMEM((own, peers, chunk, latents), F32),
        pltpu.VMEM((own, chunk, latents), F32),
        pltpu.VMEM((own, max(chunk, 128), latents), F32),
        pltpu.VMEM((layers, tokens, latents), BF16),
        pltpu.VMEM((2, tokens, width), BF16),
        pltpu.VMEM((n_z, own, tokens, latents), F32),
        pltpu.VMEM((n_z, own, half, latents), F32),
        pltpu.VMEM((n_z, own, half, latents), BF16),
        pltpu.VMEM((n_z, peers, own, chunk, latents), BF16),
        pltpu.VMEM((others, own, chunk, latents), BF16),
        pltpu.VMEM((others, own, chunk, latents), BF16),
        pltpu.VMEM((own, tokens, latents), BF16),
        pltpu.VMEM((pairs, latents, width), BF16),
        pltpu.VMEM((own, width, latents), F32),
        pltpu.SMEM((layers,), jnp.int32),
        pltpu.SMEM((layers,), jnp.int32),
        pltpu.SMEM((pairs,), jnp.int32),
        dma((2 * own + 4,)),
        dma((pairs + own,)),
    ]
    for shape in (
        (own,), (own, peers), (others, own), (n_z, own, peers), (n_z,),
        (n_z,), (n_z, peers, own), (others, own), (peers, own), (own,),
    ):
        scratch += [dma(shape), dma(shape)]
    hbm = pl.BlockSpec(memory_space=pl.ANY)
    grads = pl.pallas_call(
        functools.partial(kernel, dims),
        out_shape=(
            jax.ShapeDtypeStruct((pairs, latents, width), BF16),
            jax.ShapeDtypeStruct((own, width, latents), F32),
        ),
        in_specs=[hbm, hbm, hbm, hbm, pl.BlockSpec(memory_space=pltpu.SMEM), hbm, hbm],
        out_specs=(hbm, hbm),
        scratch_shapes=scratch,
        compiler_params=pltpu.CompilerParams(
            collective_id=0, has_side_effects=True, vmem_limit_bytes=56 * 1024 * 1024
        ),
        cost_estimate=pl.CostEstimate(
            flops=2 * tokens * width * latents * (4 * pairs + 2 * own),
            bytes_accessed=2 * (2 * pairs * latents * width + 4 * tokens * width * own),
            transcendentals=0,
        ),
        name="transcoder_step",
    )(
        source_acts, enc_weight, enc_offset, jnp.swapaxes(topk_latents, 1, 2), pair_table.T,
        dec_weight, target_acts,
    )
    return write_out(*grads)


def write_kernel(dec_in, enc_in, dec_out, enc_out, dec, enc, in_sem, out_sem):
    pairs, own = dec.shape[0], enc.shape[0]
    moves = [(dec_in.at[p], dec.at[p], dec_out.at[p]) for p in range(pairs)]
    moves += [(enc_in.at[l], enc.at[l], enc_out.at[l]) for l in range(own)]
    loads = [pltpu.make_async_copy(a, b, in_sem.at[i]) for i, (a, b, _) in enumerate(moves)]
    stores = [pltpu.make_async_copy(b, c, out_sem.at[i]) for i, (_, b, c) in enumerate(moves)]
    for load in loads:
        load.start()
    for load, store in zip(loads, stores):
        load.wait()
        store.start()
    for store in stores:
        store.wait()


def write_out(dec, enc):
    hbm = pl.BlockSpec(memory_space=pl.ANY)
    return pl.pallas_call(
        write_kernel,
        out_shape=(
            jax.ShapeDtypeStruct(dec.shape, dec.dtype), jax.ShapeDtypeStruct(enc.shape, enc.dtype)
        ),
        in_specs=[hbm, hbm],
        out_specs=(hbm, hbm),
        scratch_shapes=[
            pltpu.VMEM(dec.shape, dec.dtype),
            pltpu.VMEM(enc.shape, enc.dtype),
            pltpu.SemaphoreType.DMA((dec.shape[0] + enc.shape[0],)),
            pltpu.SemaphoreType.DMA((dec.shape[0] + enc.shape[0],)),
        ],
        compiler_params=pltpu.CompilerParams(vmem_limit_bytes=56 * 1024 * 1024),
        name="write_out",
    )(dec, enc)


def solution(mesh):
    in_specs = (
        P("layer", "groups", ("token", "width")),
        P("layer", ("token", "width"), None),
        P("layer", None),
        P("layer", "groups", None),
        P("layer", None),
        P("layer", None, ("token", "width")),
        P("layer", "groups", ("token", "width")),
    )
    out_specs = (
        P(("groups", "layer"), None, ("token", "width")),
        P(("groups", "layer"), ("token", "width"), None),
    )
    body = functools.partial(shards, mesh.shape["layer"], mesh.shape["token"])
    return jax.shard_map(body, mesh=mesh, in_specs=in_specs, out_specs=out_specs, check_vma=False)
```

```python
import functools

import jax
import jax.numpy as jnp
from jax import lax
from jax.experimental import pallas as pl
from jax.experimental.pallas import tpu as pltpu
from jax.sharding import PartitionSpec as P

grad_scale = 1.0 / 32.0
MESH = pl.DeviceIdType.MESH
F32 = jnp.float32
BF16 = jnp.bfloat16


def kernel(
    dims,
    source_hbm, encw_hbm, offset_hbm, topk_hbm, table, decw_hbm, target_hbm,
    decgrad_hbm, encgrad_hbm,
    source, source_t, encw, offset, topk, decw, target,
    part, part_core, part_x, preact, picked, lat, err,
    back, back_core, back_xs, back_x, back_zs, back_z, pre_grad, dec_out, enc_out,
    high_pair, low_pair, slot_of,
    in_sem, out_sem,
    pc_s, pc_r, px_s, px_r, lz_s, lz_r, lx_s, lx_r, lc_s, lc_r,
    bc_s, bc_r, bx_s, bx_r, bz_s, bz_r, gx_s, gx_r, gc_s, gc_r,
):
    layers, n_z, n_t, own, tokens, width, latents, pairs = dims
    half = tokens // 2
    chunk = half // n_t
    z = lax.axis_index("layer")
    t = lax.axis_index("token")
    w = lax.axis_index("width")
    other = 1 - w

    def half_rows(core):
        return pl.ds(pl.multiple_of(core * half, half), half)

    def chunk_rows(tok, core):
        return pl.ds(pl.multiple_of(core * half + tok * chunk, chunk), chunk)

    def x_peer(d):
        return lax.rem(t + d, n_t)

    def z_peer(d):
        return lax.rem(z + d, n_z)

    def z_from(d):
        return lax.rem(z - d + n_z, n_z)

    def z_layers(zz):
        return pl.ds(zz * own, own)

    my_half = half_rows(w)
    my_rows = chunk_rows(t, w)
    sends = []

    def remote(src, dst, ssem, rsem, **where):
        copy = pltpu.make_async_remote_copy(
            src_ref=src, dst_ref=dst, send_sem=ssem, recv_sem=rsem,
            device_id=where, device_id_type=MESH,
        )
        copy.start()
        sends.append(copy)
        return copy

    loads = {}

    def load(name, src, dst, sem):
        loads[name] = pltpu.make_async_copy(src, dst, in_sem.at[sem])
        loads[name].start()

    for l in range(own):
        load(("s", l), source_hbm.at[l], source.at[l], 2 * l)
        load(("e", l), encw_hbm.at[l], encw.at[l], 2 * l + 1)
    load("topk", topk_hbm, topk, 2 * own)
    load("offset", offset_hbm, offset, 2 * own + 1)
    load("decw", decw_hbm, decw.at[pl.ds(0, pairs)], 2 * own + 2)
    load("target", target_hbm, target, 2 * own + 3)

    barrier = pltpu.get_barrier_semaphore()
    pl.semaphore_signal(barrier, inc=1, device_id={"width": other}, device_id_type=MESH)
    for d in range(1, n_t):
        pl.semaphore_signal(barrier, inc=1, device_id={"token": x_peer(d)}, device_id_type=MESH)
    for d in range(1, n_z):
        pl.semaphore_signal(barrier, inc=1, device_id={"layer": z_peer(d)}, device_id_type=MESH)

    core_copies = []
    for l in range(own):
        loads[("s", l)].wait()
        loads[("e", l)].wait()
        part[l] = jnp.dot(source[l], encw[l], preferred_element_type=F32)
    pl.semaphore_wait(barrier, n_t + n_z - 1)
    for l in range(own):
        core_copies.append(remote(
            part.at[l, half_rows(other)], part_core.at[l], pc_s.at[l], pc_r.at[l], width=other))
    first_copies = []
    for l in range(own):
        core_copies[l].wait_recv()
        part[l, my_half, :] = part[l, my_half, :] + part_core[l]
        for d in range(1, n_t):
            first_copies.append(remote(
                part.at[l, chunk_rows(x_peer(d), w)], part_x.at[l, d - 1],
                px_s.at[l, d - 1], px_r.at[l, d - 1], token=x_peer(d)))

    loads["topk"].wait()
    loads["offset"].wait()
    span = picked.shape[1]
    first_row = w * half + t * chunk
    start = first_row // span * span
    mask_rows = pl.ds(pl.multiple_of(first_row - start, chunk), chunk)
    for l in range(own):
        ids = topk[l, :, pl.ds(pl.multiple_of(start, span), span)]
        names = lax.broadcasted_iota(jnp.int32, (latents, span), 0)
        hit = jnp.zeros((latents, span), F32)
        for k in range(topk.shape[1]):
            hit = jnp.where(ids[k : k + 1, :] == names, 1.0, hit)
        picked[l] = hit.T

    high_target = table[1, 0]
    for p in range(1, pairs):
        high_target = jnp.maximum(high_target, table[1, p])
    for p in range(pairs):
        slot_of[p] = (table[1, p] == high_target).astype(jnp.int32)

    @pl.loop(0, layers)
    def _(l):
        high = jnp.int32(pairs)
        low = jnp.int32(pairs)
        for p in range(pairs):
            same = table[0, p] == l
            up = table[1, p] == high_target
            high = jnp.where(jnp.logical_and(same, up), p, high)
            low = jnp.where(jnp.logical_and(same, jnp.logical_not(up)), p, low)
        high_pair[l] = high
        low_pair[l] = low

    z_copies = {}
    x_copies = {}

    def pass_x(j, l):
        for d in range(1, n_t):
            here = lat.at[z_from(j) * own + l, my_rows]
            x_copies[j, l, d] = remote(
                here, here, lx_s.at[j, l, d - 1], lx_r.at[j, l, d - 1], token=x_peer(d))

    for l in range(own):
        pre = part[l, my_rows, :] + offset[pl.ds(l, 1), :]
        for d in range(1, n_t):
            first_copies[l * (n_t - 1) + d - 1].wait_recv()
            pre = pre + part_x[l, d - 1]
        preact[l] = pre
        soft = jnp.maximum(pre, 0.0) + jnp.log1p(jnp.exp(-jnp.abs(pre)))
        lat[z * own + l, my_rows, :] = (picked[l, mask_rows, :] * soft).astype(BF16)

        for d in range(1, n_z):
            here = lat.at[z * own + l, my_rows]
            z_copies[d, l] = remote(
                here, here, lz_s.at[d - 1, l], lz_r.at[d - 1, l], layer=z_peer(d))
        pass_x(0, l)
    for l in range(own):
        source_t[l] = source[l].T
    loads["decw"].wait()
    decw[pairs] = jnp.zeros((latents, width), BF16)
    loads["target"].wait()
    for j in range(1, n_z):
        for l in range(own):
            z_copies[j, l].wait_recv()
            pass_x(j, l)
    core_copies = []
    for j in range(n_z):
        for l in range(own):
            for d in range(1, n_t):
                x_copies[j, l, d].wait_recv()
        here = lat.at[z_layers(z_from(j)), my_half]
        core_copies.append(remote(here, here, lc_s.at[j], lc_r.at[j], width=other))
    tile = 256
    lows = layers // 2

    def decode(rows):
        @pl.loop(0, width // tile)
        def _(n):
            cols = pl.ds(pl.multiple_of(n * tile, tile), tile)
            for slot, count, pair_of in ((1, layers, high_pair), (0, lows, low_pair)):
                acts = jnp.concatenate([lat[l, rows, :] for l in range(count)], axis=1)
                weight = jnp.concatenate([decw[pair_of[l], :, cols] for l in range(count)], axis=0)
                rebuilt = jnp.dot(acts, weight, preferred_element_type=F32)
                goal = target[slot, rows, cols].astype(F32)
                err[slot, rows, cols] = ((rebuilt - goal) * grad_scale).astype(BF16)

    decode(my_half)
    for j in range(n_z):
        core_copies[j].wait_recv()
    decode(half_rows(other))

    order = [n_z // 2] + [j for j in range(1, n_z) if j != n_z // 2] + [0]
    core_copies = {}
    x_copies = {}
    z_copies = {}

    def spread_to(j):
        zz = z_peer(j)
        def times(slot, pair_of, rows):
            weight = jnp.concatenate([decw[pair_of[zz * own + i]] for i in range(own)], axis=0)
            return lax.dot_general(
                err[slot, rows, :], weight, (((1,), (1,)), ((), ())), preferred_element_type=F32)

        def half_spread(rows):
            spread = times(1, high_pair, rows)
            for i in range(own):
                back[j, i, rows, :] = spread[:, i * latents : (i + 1) * latents]

            @pl.when(zz * own < lows)
            def _():
                spread = times(0, low_pair, rows)
                for i in range(own):
                    back[j, i, rows, :] = (
                        back[j, i, rows, :] + spread[:, i * latents : (i + 1) * latents])

        half_spread(half_rows(other))
        core_copies[j] = remote(
            back.at[j, :, half_rows(other)], back_core.at[j], bc_s.at[j], bc_r.at[j], width=other)
        half_spread(my_half)

    def send_x(j):
        core_copies[j].wait_recv()
        for i in range(own):
            total = back[j, i, my_half, :] + back_core[j, i]
            back[j, i, my_half, :] = total
            back_xs[j, i] = total.astype(BF16)
            for d in range(1, n_t):
                rows = pl.ds(pl.multiple_of(x_peer(d) * chunk, chunk), chunk)
                x_copies[j, i, d] = remote(
                    back_xs.at[j, i, rows], back_x.at[j, d - 1, i],
                    bx_s.at[j, d - 1, i], bx_r.at[j, d - 1, i], token=x_peer(d))

    def send_z(j):
        totals = []
        for i in range(own):
            total = back[j, i, my_rows, :]
            for d in range(1, n_t):
                x_copies[j, i, d].wait_recv()
                total = total + back_x[j, d - 1, i].astype(F32)
            totals.append(total)
            if j:
                back_zs[j - 1, i] = total.astype(BF16)
                z_copies[j, i] = remote(
                    back_zs.at[j - 1, i], back_z.at[j - 1, i],
                    bz_s.at[j - 1, i], bz_r.at[j - 1, i], layer=z_peer(j))
        return totals

    def dec_gradient(first, last):
        @pl.loop(first, last)
        def _(p):
            acts = lat[table[0, p]].T
            grad = jnp.dot(acts, err[slot_of[p]], preferred_element_type=F32)
            dec_out[p] = grad.astype(BF16)
            pltpu.make_async_copy(dec_out.at[p], decgrad_hbm.at[p], out_sem.at[p]).start()

    spread_to(order[0])
    for step in range(1, n_z):
        spread_to(order[step])
        send_x(order[step - 1])
    send_x(order[-1])
    for step in range(n_z):
        mine = send_z(order[step])
        dec_gradient(step * pairs // n_z, (step + 1) * pairs // n_z)
    g_copies = {}
    for l in range(own):
        grad = mine[l]
        for j in range(1, n_z):
            z_copies[j, l].wait_recv()
            grad = grad + back_z[j - 1, l].astype(F32)
        pre_grad[l, my_rows, :] = (
            grad * picked[l, mask_rows, :] * jax.nn.sigmoid(preact[l])).astype(BF16)
        here = pre_grad.at[l, my_rows]
        for d in range(1, n_t):
            g_copies[l, d] = remote(
                here, here, gx_s.at[d - 1, l], gx_r.at[d - 1, l], token=x_peer(d))
    core_copies = []
    for l in range(own):
        for d in range(1, n_t):
            g_copies[l, d].wait_recv()
        here = pre_grad.at[l, my_half]
        core_copies.append(remote(here, here, gc_s.at[l], gc_r.at[l], width=other))
    for l in range(own):
        enc_out[l] = jnp.dot(
            source_t[l, :, my_half], pre_grad[l, my_half, :], preferred_element_type=F32)
    rest = half_rows(other)
    for l in range(own):
        core_copies[l].wait_recv()
        enc_out[l] = enc_out[l] + jnp.dot(
            source_t[l, :, rest], pre_grad[l, rest, :], preferred_element_type=F32)
        pltpu.make_async_copy(enc_out.at[l], encgrad_hbm.at[l], out_sem.at[pairs + l]).start()
    for copy in sends:
        copy.wait_send()

    @pl.loop(0, pairs)
    def _(p):
        pltpu.make_async_copy(dec_out.at[p], decgrad_hbm.at[p], out_sem.at[p]).wait()

    for l in range(own):
        pltpu.make_async_copy(enc_out.at[l], encgrad_hbm.at[l], out_sem.at[pairs + l]).wait()


def shards(n_z, n_t, source_acts, enc_weight, enc_offset, topk_latents, pair_table, dec_weight, target_acts):
    own, tokens, width = source_acts.shape
    latents = enc_weight.shape[2]
    pairs = pair_table.shape[0]
    topk = topk_latents.shape[2]
    layers = own * n_z
    half = tokens // 2
    chunk = half // n_t
    peers = max(n_t - 1, 1)
    others = max(n_z - 1, 1)
    dims = (layers, n_z, n_t, own, tokens, width, latents, pairs)
    dma = pltpu.SemaphoreType.DMA
    scratch = [
        pltpu.VMEM((own, tokens, width), BF16),
        pltpu.VMEM((own, width, tokens), BF16),
        pltpu.VMEM((own, width, latents), BF16),
        pltpu.VMEM((own, latents), F32),
        pltpu.VMEM((own, topk, tokens), jnp.int32),
        pltpu.VMEM((pairs + 1, latents, width), BF16),
        pltpu.VMEM((2, tokens, width), BF16),
        pltpu.VMEM((own, tokens, latents), F32),
        pltpu.VMEM((own, half, latents), F32),
        pltpu.VMEM((own, peers, chunk, latents), F32),
        pltpu.VMEM((own, chunk, latents), F32),
        pltpu.VMEM((own, max(chunk, 128), latents), F32),
        pltpu.VMEM((layers, tokens, latents), BF16),
        pltpu.VMEM((2, tokens, width), BF16),
        pltpu.VMEM((n_z, own, tokens, latents), F32),
        pltpu.VMEM((n_z, own, half, latents), F32),
        pltpu.VMEM((n_z, own, half, latents), BF16),
        pltpu.VMEM((n_z, peers, own, chunk, latents), BF16),
        pltpu.VMEM((others, own, chunk, latents), BF16),
        pltpu.VMEM((others, own, chunk, latents), BF16),
        pltpu.VMEM((own, tokens, latents), BF16),
        pltpu.VMEM((pairs, latents, width), BF16),
        pltpu.VMEM((own, width, latents), F32),
        pltpu.SMEM((layers,), jnp.int32),
        pltpu.SMEM((layers,), jnp.int32),
        pltpu.SMEM((pairs,), jnp.int32),
        dma((2 * own + 4,)),
        dma((pairs + own,)),
    ]
    for shape in (
        (own,), (own, peers), (others, own), (n_z, own, peers), (n_z,),
        (n_z,), (n_z, peers, own), (others, own), (peers, own), (own,),
    ):
        scratch += [dma(shape), dma(shape)]
    hbm = pl.BlockSpec(memory_space=pl.ANY)
    grads = pl.pallas_call(
        functools.partial(kernel, dims),
        out_shape=(
            jax.ShapeDtypeStruct((pairs, latents, width), BF16),
            jax.ShapeDtypeStruct((own, width, latents), F32),
        ),
        in_specs=[hbm, hbm, hbm, hbm, pl.BlockSpec(memory_space=pltpu.SMEM), hbm, hbm],
        out_specs=(hbm, hbm),
        scratch_shapes=scratch,
        compiler_params=pltpu.CompilerParams(
            collective_id=0, has_side_effects=True, vmem_limit_bytes=56 * 1024 * 1024
        ),
        cost_estimate=pl.CostEstimate(
            flops=2 * tokens * width * latents * (4 * pairs + 2 * own),
            bytes_accessed=2 * (2 * pairs * latents * width + 4 * tokens * width * own),
            transcendentals=0,
        ),
        name="transcoder_step",
    )(
        source_acts, enc_weight, enc_offset, jnp.swapaxes(topk_latents, 1, 2), pair_table.T,
        dec_weight, target_acts,
    )
    return write_out(*grads)


def write_kernel(dec_in, enc_in, dec_out, enc_out, dec, enc, in_sem, out_sem):
    pairs, own = dec.shape[0], enc.shape[0]
    moves = [(dec_in.at[p], dec.at[p], dec_out.at[p]) for p in range(pairs)]
    moves += [(enc_in.at[l], enc.at[l], enc_out.at[l]) for l in range(own)]
    loads = [pltpu.make_async_copy(a, b, in_sem.at[i]) for i, (a, b, _) in enumerate(moves)]
    stores = [pltpu.make_async_copy(b, c, out_sem.at[i]) for i, (_, b, c) in enumerate(moves)]
    for load in loads:
        load.start()
    for load, store in zip(loads, stores):
        load.wait()
        store.start()
    for store in stores:
        store.wait()


def write_out(dec, enc):
    hbm = pl.BlockSpec(memory_space=pl.ANY)
    return pl.pallas_call(
        write_kernel,
        out_shape=(
            jax.ShapeDtypeStruct(dec.shape, dec.dtype), jax.ShapeDtypeStruct(enc.shape, enc.dtype)
        ),
        in_specs=[hbm, hbm],
        out_specs=(hbm, hbm),
        scratch_shapes=[
            pltpu.VMEM(dec.shape, dec.dtype),
            pltpu.VMEM(enc.shape, enc.dtype),
            pltpu.SemaphoreType.DMA((dec.shape[0] + enc.shape[0],)),
            pltpu.SemaphoreType.DMA((dec.shape[0] + enc.shape[0],)),
        ],
        compiler_params=pltpu.CompilerParams(vmem_limit_bytes=56 * 1024 * 1024),
        name="write_out",
    )(dec, enc)


def solution(mesh):
    in_specs = (
        P("layer", "groups", ("token", "width")),
        P("layer", ("token", "width"), None),
        P("layer", None),
        P("layer", "groups", None),
        P("layer", None),
        P("layer", None, ("token", "width")),
        P("layer", "groups", ("token", "width")),
    )
    out_specs = (
        P(("groups", "layer"), None, ("token", "width")),
        P(("groups", "layer"), ("token", "width"), None),
    )
    body = functools.partial(shards, mesh.shape["layer"], mesh.shape["token"])
    return jax.shard_map(body, mesh=mesh, in_specs=in_specs, out_specs=out_specs, check_vma=False)
```
